32 devices in a mesh: lon: 2 (over x), sec: 4 (over y, core), rad: 4 (over z).
Axes of the slice: x: 2, y: 2, z: 4, core: 2. Of those that a mesh axis runs over, the one named last changes fastest.
Arguments:
- plasma_fields: float32 [8, 64, 8, 512], P(None, 'sec', 'lon', 'rad'), may hold values from -6 to 6
- velocity: bfloat16 [3, 64, 8, 512], P(None, 'sec', 'lon', 'rad'), may hold values from -1 to 1
- resistivity: bfloat16 [64, 8, 512], P('sec', 'lon', 'rad'), may hold values from 0.0049743652 to 0.039794922
- conductance: float32 [8, 512], P('lon', 'rad'), may hold values from 0.5 to 5
- foot_map: int32 [4096, 256], P(('lon', 'sec', 'rad')), may hold values from 0 to 511
- foot_owner: int32 [4096, 1], P(('lon', 'sec', 'rad')), may hold values from 0 to 7; in each aligned block of 128 rows (0 to 127, 128 to 255, ...) at most 32 rows name the same one
- foot_row: int32 [4096], P(('lon', 'sec', 'rad')), may hold values from 0 to 31
Outputs:
- advanced_fields: float32 [8, 64, 8, 512], P(None, 'sec', 'lon', 'rad')
- potential: float32 [8, 512], P('lon', 'rad')
- foot_table: float32 [1024, 256], P(('lon', 'sec', 'rad'))
The draws below stay inside these ranges and needn't reach their ends.
Inputs may be any that keep to these rules, and one draw needn't show every extreme that they name: `foot_owner`: in each aligned block of 128 rows (the records of one device) no owner index appears more than 32 times.
All inputs are finite; a program needn't handle non-finite values.
Results may differ from the reference program's by a relative error of at most 0.0003.
Values sent between devices are 32-bit elements; how exact they have to be, the bound alone decides.
A program may use at most 128 MiB of HBM per device.

```python
import math
import jax
import jax.numpy as jnp
import numpy as np
from jax import lax

LON_DEV = 4
LAT_DEV = 128
PHASES = 4
SWEEPS = 8
POINTS = 256
REC_DEV = 128
ROWS_OWN = 32
NR = 64
NLON = 8
NLAT = 512
RECORDS = 4096
CAP = 32
N_LON = 2
N_SEC = 4
N_RAD = 4


def plant(values, stream_key, smallest, high):
    shape = values.shape
    index_at = [jax.random.randint(jax.random.fold_in(stream_key, axis), (), 0, shape[axis]) for axis in range(len(shape))]
    values = values.at[tuple(index_at)].set(smallest)
    longest = shape.index(max(shape))
    index_at[longest] = (index_at[longest] + 1) % shape[longest]
    return values.at[tuple(index_at)].set(high)


def level_of(rng, dims, shards, least, largest):
    def one(dim, blocks):
        draws = jax.random.uniform(jax.random.fold_in(jax.random.fold_in(rng, 6), dim), (blocks,), jnp.float32, least / len(shards), largest / len(shards))
        return jnp.repeat(jnp.exp(draws), dims[dim] // blocks).reshape((-1,) + (1,) * (len(dims) - dim - 1))

    factor_of = one(*shards[0])
    for cut in shards[1:]:
        factor_of = factor_of * one(*cut)
    return factor_of


def shared_out(own_key, own, number, rows, amount, top, reach, lean):
    sequence = jax.random.permutation(own_key, amount)
    heavy_load, common = shares(amount, rows * top, reach, lean, True), shares(amount, rows * top, reach, lean, False)
    places = jnp.arange(amount)

    def named(lengths, turn):
        used = int((lengths > 0).sum())
        fixed = max(1, used // 4)
        passed = fixed + (places - fixed + turn * (used - fixed)) % max(1, amount - fixed)
        return jnp.zeros((amount,), jnp.int32).at[sequence[jnp.where(places < fixed, places, passed)]].set(jnp.asarray(lengths, jnp.int32))

    lengths = jnp.where(number % 4 == 0, named(heavy_load, number // 4), named(common, number - number // 4 - 1))
    mixed = jax.random.permutation(jax.random.fold_in(own, 3), amount)
    giver, taker = mixed[0:amount // 2 * 2:2], mixed[1:amount // 2 * 2:2]
    room = jnp.minimum(lengths[giver] - 1, reach - lengths[taker]) // 2
    room = jnp.where((giver == sequence[0]) | (taker == sequence[0]) | (lengths[taker] == 0), 0, jnp.maximum(room, 0))
    passed = jax.random.randint(jax.random.fold_in(own, 4), (amount // 2,), 0, 1 << 20) % (room + 1)
    lengths = lengths.at[giver].add(-passed).at[taker].add(passed)
    members = jnp.searchsorted(jnp.cumsum(lengths), jnp.arange(rows * top), side="right").astype(jnp.int32)
    table = members.reshape(top, rows).T
    table = table[jax.random.permutation(jax.random.fold_in(own, 1), rows)]
    turn = jax.random.randint(jax.random.fold_in(own, 2), (rows, 1), 0, top)
    return jnp.take_along_axis(table, (jnp.arange(top)[None, :] + turn) % top, axis=1)


def shares(amount, total, bound, skew, full):
    portions = [(1 << 20) // math.isqrt(standing ** skew) + 1 for standing in range(1, amount + 1)]
    largest = bound if full else min(bound, max(-(-total // amount), total * portions[0] // sum(portions)))
    least = 1 if total - largest >= amount - 1 else 0
    given, spare = [largest] + [least] * (amount - 1), total - largest - least * (amount - 1)
    while spare > 0:
        movable = [i for i in range(1, amount) if given[i] < largest] or [i for i in range(1, amount) if given[i] < bound]
        mass, remaining = sum([portions[i] for i in movable]), spare
        for i in movable:
            more = min(bound - given[i], max(1, remaining * portions[i] // mass), spare)
            given[i] = given[i] + more
            spare = spare - more
    return np.array(given)


def bell_draw(own_key, extent, scale, limit, pieces=(), held_as=jnp.bfloat16):
    drawn = jax.random.normal(own_key, extent, jnp.float32) * scale
    if len(pieces) > 0:
        drawn = level_of(own_key, extent, pieces, -0.22, 0.18) * drawn
    return jnp.clip(drawn, min=-limit, max=limit).astype(held_as)


def setup_inputs(seed: int = 0) -> dict:
    arg_keys = jax.random.split(jax.random.key(seed), 8)
    plasma_fields = bell_draw(arg_keys[0], (8, NR, NLON, NLAT), 1.0, 6.0, ((1, 4), (2, 2), (3, 4)), jnp.float32)
    velocity = jnp.clip(jax.random.uniform(arg_keys[1], (3, NR, NLON, NLAT), jnp.float32, -1.0, 1.0) * level_of(arg_keys[1], (3, NR, NLON, NLAT), ((1, 4), (2, 2), (3, 4)), -0.4, 0.0), -1.0, 1.0).astype(jnp.bfloat16)
    resistivity = jnp.clip(jnp.exp(math.log(0.039794922) - 2.0794415 * jax.random.uniform(arg_keys[2], (NR, NLON, NLAT), jnp.float32) ** level_of(arg_keys[2], (NR, NLON, NLAT), ((0, 4), (1, 2), (2, 4)), -0.2, 0.2)), 0.0049743652, 0.039794922).astype(jnp.bfloat16)
    conductance = jnp.clip(jnp.exp(math.log(5.0) - 2.3025851 * jax.random.uniform(arg_keys[3], (NLON, NLAT), jnp.float32) ** level_of(arg_keys[3], (NLON, NLAT), ((0, 2), (1, 4)), -0.2, 0.2)), 0.5, 5.0)
    foot_map = plant(jax.random.randint(arg_keys[4], (RECORDS, POINTS), 0, LON_DEV * LAT_DEV), jax.random.fold_in(arg_keys[4], 1), 0, (LON_DEV * LAT_DEV) - 1).astype(jnp.int32)
    foot_owner_keys = jax.random.split(jax.random.fold_in(arg_keys[5], 1), RECORDS // REC_DEV)
    foot_owner_turns = jax.random.permutation(jax.random.fold_in(arg_keys[5], 3), RECORDS // REC_DEV)
    foot_owner = jax.vmap(lambda own, number: shared_out(jax.random.fold_in(arg_keys[5], 2), own, number, REC_DEV, N_LON * N_RAD, 1, CAP, 2))(foot_owner_keys, foot_owner_turns).reshape((RECORDS, 1))
    foot_row = plant(jax.random.randint(arg_keys[6], (RECORDS,), 0, ROWS_OWN), jax.random.fold_in(arg_keys[6], 1), 0, ROWS_OWN - 1).astype(jnp.int32)
    return {"plasma_fields": plasma_fields, "velocity": velocity, "resistivity": resistivity, "conductance": conductance, "foot_map": foot_map, "foot_owner": foot_owner, "foot_row": foot_row}


COURANT = 0.25
DAMPING = 0.05
RELAX = 0.8


def advance(padded, velocity_f, resist_f):
    centre = padded[:, 1:-1, 1:-1, 1:-1]
    shell_lo = padded[:, :-2, 1:-1, 1:-1]
    shell_hi = padded[:, 2:, 1:-1, 1:-1]
    lon_lo = padded[:, 1:-1, :-2, 1:-1]
    lon_hi = padded[:, 1:-1, 2:, 1:-1]
    lat_lo = padded[:, 1:-1, 1:-1, :-2]
    lat_hi = padded[:, 1:-1, 1:-1, 2:]

    def upwind(component, lower_side, upper_side):
        return jnp.maximum(component, 0.0) * (centre - lower_side) + jnp.minimum(component, 0.0) * (upper_side - centre)

    transport = upwind(velocity_f[0], shell_lo, shell_hi) + upwind(velocity_f[1], lon_lo, lon_hi) + upwind(velocity_f[2], lat_lo, lat_hi)
    spread = shell_lo + shell_hi + lon_lo + lon_hi + lat_lo + lat_hi - 6.0 * centre
    return centre - COURANT * transport + resist_f * spread


def frame_plane(values):
    wrapped = jnp.concatenate([values[..., -1:, :], values, values[..., :1, :]], axis=-2)
    widths = [(0, 0)] * (values.ndim - 1) + [(1, 1)]
    return jnp.pad(wrapped, widths)


def reference(plasma_fields, velocity, resistivity, conductance, foot_map, foot_owner, foot_row):
    velocity_f = velocity.astype(jnp.float32)
    resist_f = resistivity.astype(jnp.float32)

    def one_field(single):
        current = single
        for step_index in range(PHASES):
            wrapped = jnp.concatenate([current[:, -1:, :], current, current[:, :1, :]], axis=1)
            padded = jnp.pad(wrapped, ((1, 1), (0, 0), (1, 1)))
            current = advance(padded[None], velocity_f, resist_f)[0]
        return current

    advanced = lax.map(one_field, plasma_fields)
    base = jnp.concatenate([advanced[5:7, 0], conductance[None]], axis=0)
    framed = frame_plane(base)
    field_lon = framed[0]
    field_lat = framed[1]
    cond_all = framed[2]
    source = (field_lat[2:, 1:-1] - field_lat[:-2, 1:-1]) - (field_lon[1:-1, 2:] - field_lon[1:-1, :-2])
    middle = cond_all[1:-1, 1:-1]
    east = 0.5 * (middle + cond_all[2:, 1:-1])
    west = 0.5 * (middle + cond_all[:-2, 1:-1])
    north = 0.5 * (middle + cond_all[1:-1, 2:])
    south = 0.5 * (middle + cond_all[1:-1, :-2])
    diagonal = DAMPING * middle + east + west + north + south
    potential = jnp.zeros_like(conductance)
    for sweep_index in range(SWEEPS):
        framed_phi = frame_plane(potential)
        centre = framed_phi[1:-1, 1:-1]
        image = diagonal * centre - (east * framed_phi[2:, 1:-1] + west * framed_phi[:-2, 1:-1] + north * framed_phi[1:-1, 2:] + south * framed_phi[1:-1, :-2])
        potential = centre + RELAX * (source - image) / diagonal
    blocks = potential.reshape(N_LON, LON_DEV, N_RAD, LAT_DEV).transpose(0, 2, 1, 3).reshape(N_LON * N_RAD, LON_DEV * LAT_DEV)
    device = (jnp.arange(RECORDS) // REC_DEV).astype(jnp.int32)
    lon_of = device // (N_SEC * N_RAD)
    sec_of = (device // N_RAD) % N_SEC
    rad_of = device % N_RAD
    records = blocks[(lon_of * N_RAD + rad_of)[:, None], foot_map]
    target = foot_owner[:, 0]
    owner = (target // N_RAD) * (N_SEC * N_RAD) + sec_of * N_RAD + target % N_RAD
    foot_table = jax.ops.segment_sum(records, owner * ROWS_OWN + foot_row, num_segments=N_LON * N_SEC * N_RAD * ROWS_OWN)
    return advanced, potential, foot_table
```

```python
import functools

import jax
import jax.numpy as jnp
from jax import lax
from jax.experimental import pallas as pl
from jax.experimental.pallas import tpu as pltpu
from jax.sharding import PartitionSpec as P

PHASES = 4
SWEEPS = 8
ROWS_OWN = 32
COURANT = 0.25
DAMPING = 0.05
RELAX = 0.8
MESH = pl.DeviceIdType.MESH
GROUPS = ((5, 7), (0, 3), (3, 5), (7, 8))


def each(count, body):
    if count <= 16:
        for i in range(count):
            body(i)
    else:
        lax.fori_loop(0, count, lambda i, c: (body(i), c)[1], 0)


def kernel(
    sizes,
    fields, vel, res, cond, fmap, fowner, frow,
    out, out_phi, out_table,
    wide, coef, cells, shell_out, shell_in, lat_out, lat_in,
    mags, conds, map_out, map_in, row_out, row_in, phis, recs, codes, select,
    halo_send, halo_recv, mag_send, mag_recv, cond_send, cond_recv, map_send, map_recv, row_send, row_recv,
):
    n_lon, n_sec, n_rad, n_fields, shells, lons, lats, cap = sizes
    me_l, me_s, me_r = lax.axis_index("lon"), lax.axis_index("sec"), lax.axis_index("rad")
    n_all, n_own = n_lon * n_sec * n_rad, n_lon * n_rad
    me_own = me_l * n_rad + me_r
    me_flat = (me_l * n_sec + me_s) * n_rad + me_r

    def place(flat):
        return (flat // (n_sec * n_rad), (flat // n_rad) % n_sec, flat % n_rad)

    def mate(owner):
        return (owner // n_rad, me_s, owner % n_rad)

    barrier = pltpu.get_barrier_semaphore()

    def greet(t, c):
        pl.semaphore_signal(barrier, inc=1, device_id=place((me_flat + t) % n_all), device_id_type=MESH)
        return c

    lax.fori_loop(1, n_all, greet, 0)

    lane = lax.broadcasted_iota(jnp.int32, (shells, lats), 1)
    lane3 = lax.broadcasted_iota(jnp.int32, (lons, shells, lats), 2)
    row3 = lax.broadcasted_iota(jnp.int32, (lons, shells, lats), 1)

    def publish(p, g, blocks):
        f0, _ = GROUPS[g]
        low = jnp.zeros((shells, lats), jnp.float32)
        high = jnp.zeros((shells, lats), jnp.float32)
        for i, block in enumerate(blocks):
            f = f0 + i
            cells[p, f, 1 : lons + 1] = block
            shell_out[p, 0, f] = block[:, 0:1, :]
            shell_out[p, 1, f] = block[:, shells - 1 : shells, :]
            for l in range(lons):
                k = i * lons + l
                low = jnp.where(lane == k, pltpu.roll(block[l], k, 1) if k else block[l], low)
                high = jnp.where(lane == k, pltpu.roll(block[l], k + 1, 1), high)
        lat_out[p, g, 0] = low
        lat_out[p, g, 1] = high

    left, right = lax.rem(me_l + n_lon - 1, n_lon), lax.rem(me_l + 1, n_lon)

    def halo(p, g, way):
        f0, f1 = GROUPS[g]
        span = pl.ds(f0, f1 - f0)
        src, dst, to = (
            (lambda: (cells.at[p, span, 1], cells.at[p, span, lons + 1], (left, me_s, me_r))),
            (lambda: (cells.at[p, span, lons], cells.at[p, span, 0], (right, me_s, me_r))),
            (lambda: (shell_out.at[p, 0, span], shell_in.at[p, 1, span], (me_l, me_s - 1, me_r))),
            (lambda: (shell_out.at[p, 1, span], shell_in.at[p, 0, span], (me_l, me_s + 1, me_r))),
            (lambda: (lat_out.at[p, g, 0], lat_in.at[p, g, 1], (me_l, me_s, me_r - 1))),
            (lambda: (lat_out.at[p, g, 1], lat_in.at[p, g, 0], (me_l, me_s, me_r + 1))),
        )[way]()
        return pltpu.make_async_remote_copy(
            src_ref=src, dst_ref=dst, send_sem=halo_send.at[p, g, way], recv_sem=halo_recv.at[p, g, way],
            device_id=to, device_id_type=MESH,
        )

    sends = (None, None, me_s > 0, me_s < n_sec - 1, me_r > 0, me_r < n_rad - 1)
    takes = (None, None, me_s < n_sec - 1, me_s > 0, me_r < n_rad - 1, me_r > 0)

    def guarded(cond_value, act):
        if cond_value is None:
            act()
        else:
            pl.when(cond_value)(act)

    def start_halo(p, g):
        for way in (0, 1, 4, 5, 2, 3):
            guarded(sends[way], lambda: halo(p, g, way).start())

    def wait_halo(p, g):
        for way in range(6):
            guarded(takes[way], lambda: halo(p, g, way).wait_recv())

    starts = []
    for g, (f0, f1) in enumerate(GROUPS):
        blocks = []
        for f in range(f0, f1):
            blocks.append(jnp.stack([fields[f, pl.ds(l, shells, stride=lons), :] for l in range(lons)]))
        publish(0, g, blocks)

    @pl.when(me_s == 0)
    def _():
        shell_in[:, 0] = jnp.zeros_like(shell_in[:, 0])

    @pl.when(me_s == n_sec - 1)
    def _():
        shell_in[:, 1] = jnp.zeros_like(shell_in[:, 1])

    @pl.when(me_r == 0)
    def _():
        lat_in[:, :, 0] = jnp.zeros_like(lat_in[:, :, 0])

    @pl.when(me_r == n_rad - 1)
    def _():
        lat_in[:, :, 1] = jnp.zeros_like(lat_in[:, :, 1])

    conds[me_own] = cond[...]

    pl.semaphore_wait(barrier, n_all - 1)

    for g in range(len(GROUPS)):
        start_halo(0, g)

    count = fmap.shape[0]
    g_row = lax.broadcasted_iota(jnp.int32, (count, count), 0)
    g_lane = lax.broadcasted_iota(jnp.int32, (count, count), 1)
    owner_c = jnp.broadcast_to(fowner[...].astype(jnp.float32), (count, count))
    row_l = jnp.broadcast_to(frow[...].astype(jnp.float32), (count, count))
    same = g_row == g_lane
    owner_l = jnp.sum(jnp.where(same, owner_c, 0.0), axis=0, keepdims=True)
    row_c = jnp.sum(jnp.where(same, row_l, 0.0), axis=1, keepdims=True)
    alike = owner_c == owner_l
    rank_l = jnp.sum(jnp.where(alike & (g_row < g_lane), 1.0, 0.0), axis=0, keepdims=True)
    rank_c = jnp.sum(jnp.where(alike & (g_row > g_lane), 1.0, 0.0), axis=1, keepdims=True)
    key_l = (owner_l * float(count) + rank_l)
    key_c = (owner_c[:, 0:1] * float(count) + rank_c)
    spot = lax.broadcasted_iota(jnp.int32, (cap, count), 0).astype(jnp.float32)
    spot_l = g_lane.astype(jnp.float32)
    ids = fmap[...]
    high_part = (ids // lats).astype(jnp.float32).astype(jnp.bfloat16)
    low_part = (ids % lats).astype(jnp.float32).astype(jnp.bfloat16)

    def gather_owner(o):
        base = jnp.asarray(o * count, jnp.int32).astype(jnp.float32)
        pick = jnp.where(spot + base == key_l, 1.0, 0.0).astype(jnp.bfloat16)
        highs = jnp.dot(pick, high_part, preferred_element_type=jnp.float32)
        lows = jnp.dot(pick, low_part, preferred_element_type=jnp.float32)
        map_out[o] = highs * float(lats) + lows
        hit = spot_l + base == key_c
        rows = jnp.sum(jnp.where(hit, row_c + 1.0, 0.0), axis=0, keepdims=True) - 1.0
        row_out[o] = jnp.broadcast_to(rows, (8, count))

    each(n_own, gather_owner)
    map_in[me_own] = map_out[me_own]
    row_in[me_own] = row_out[me_own]

    def to_mate(t, src, dst, send, recv):
        o = (me_own + t) % n_own
        return pltpu.make_async_remote_copy(
            src_ref=src(o), dst_ref=dst.at[me_own], send_sem=send.at[t], recv_sem=recv.at[t],
            device_id=mate(o), device_id_type=MESH,
        )

    def cond_copy(t):
        return to_mate(t, lambda o: conds.at[me_own], conds, cond_send, cond_recv)

    def map_copy(t):
        return to_mate(t, lambda o: map_out.at[o], map_in, map_send, map_recv)

    def row_copy(t):
        return to_mate(t, lambda o: row_out.at[o], row_in, row_send, row_recv)

    def start_mates(t, c):
        cond_copy(t).start()
        row_copy(t).start()
        map_copy(t).start()
        return c

    lax.fori_loop(1, n_own, start_mates, 0)

    wide[0:3] = vel[...].astype(jnp.float32)
    wide[3] = res[...].astype(jnp.float32)
    for l in range(lons):
        w = [wide[d, pl.ds(l, shells, stride=lons), :] for d in range(3)]
        r = wide[3, pl.ds(l, shells, stride=lons), :]
        middle = 1.0 - 6.0 * r
        for d in range(3):
            up = COURANT * jnp.maximum(w[d], 0.0)
            down = COURANT * jnp.minimum(w[d], 0.0)
            coef[1 + 2 * d, l] = r + up
            coef[2 + 2 * d, l] = r - down
            middle = middle - (up - down)
        coef[0, l] = middle

    def step(p, g, i):
        f = GROUPS[g][0] + i
        here = cells[p, f, 1 : lons + 1]
        total = coef[0] * here
        total += coef[3] * cells[p, f, 0:lons] + coef[4] * cells[p, f, 2 : lons + 2]
        lower = jnp.where(row3 == 0, shell_in[p, 0, f], pltpu.roll(here, 1, 1))
        upper = jnp.where(row3 == shells - 1, shell_in[p, 1, f], pltpu.roll(here, shells - 1, 1))
        total += coef[1] * lower + coef[2] * upper
        low_edge, high_edge = lat_in[p, g, 0], lat_in[p, g, 1]
        ks = [i * lons + l for l in range(lons)]
        low_edges = jnp.stack([pltpu.roll(low_edge, lats - k, 1) if k else low_edge for k in ks])
        high_edges = jnp.stack([pltpu.roll(high_edge, lats - 1 - k, 1) for k in ks])
        lower = jnp.where(lane3 == 0, low_edges, pltpu.roll(here, 1, 2))
        upper = jnp.where(lane3 == lats - 1, high_edges, pltpu.roll(here, lats - 1, 2))
        return total + coef[5] * lower + coef[6] * upper

    def mag_copy(t):
        return pltpu.make_async_remote_copy(
            src_ref=mags.at[me_own], dst_ref=mags.at[me_own], send_sem=mag_send.at[t],
            recv_sem=mag_recv.at[me_own], device_id=place((me_flat + t) % n_all), device_id_type=MESH,
        )

    for p in range(PHASES):
        for g, (f0, f1) in enumerate(GROUPS):
            wait_halo(p, g)
            blocks = [step(p, g, i) for i in range(f1 - f0)]
            if p < PHASES - 1:
                publish(p + 1, g, blocks)
                start_halo(p + 1, g)
                continue
            if g == 0:

                @pl.when(me_s == 0)
                def _():
                    for c in range(2):
                        for l in range(lons):
                            mags[me_own, c, l : l + 1, :] = blocks[c][l, 0:1, :]

                    def send_mag(t, c):
                        mag_copy(t).start()
                        return c

                    lax.fori_loop(1, n_all, send_mag, 0)

            for i in range(f1 - f0):
                for l in range(lons):
                    out[f0 + i, pl.ds(l, shells, stride=lons), :] = blocks[i][l]

    def wait_mates(t, c):
        cond_copy(t).wait_recv()
        row_copy(t).wait_recv()
        map_copy(t).wait_recv()
        return c

    lax.fori_loop(1, n_own, wait_mates, 0)

    def whole(get):
        return jnp.concatenate(
            [jnp.concatenate([get(i * n_rad + j) for j in range(n_rad)], axis=1) for i in range(n_lon)], axis=0
        )

    nl, nt = n_lon * lons, n_rad * lats
    t_full = lax.broadcasted_iota(jnp.int32, (nl, nt), 1)

    def lon_up(x):
        return pltpu.roll(x, nl - 1, 0)

    def lon_down(x):
        return pltpu.roll(x, 1, 0)

    def lat_up(x):
        return jnp.where(t_full == nt - 1, 0.0, pltpu.roll(x, nt - 1, 1))

    def lat_down(x):
        return jnp.where(t_full == 0, 0.0, pltpu.roll(x, 1, 1))

    c_full = whole(lambda o: conds[o])
    east = 0.5 * (c_full + lon_up(c_full))
    west = 0.5 * (c_full + lon_down(c_full))
    north = 0.5 * (c_full + lat_up(c_full))
    south = 0.5 * (c_full + lat_down(c_full))
    scale = RELAX / (DAMPING * c_full + east + west + north + south)
    east, west, north, south = east * scale, west * scale, north * scale, south * scale

    rows_at = lax.broadcasted_iota(jnp.int32, (ROWS_OWN, count), 0).astype(jnp.float32)
    per = count // cap
    for b in range(n_own // per if n_own >= per else 1):
        part = jnp.zeros((ROWS_OWN, count), jnp.float32)
        for s in range(b * per, min((b + 1) * per, n_own)):
            one = jnp.where(rows_at == row_in[s][0:1, :], 1.0, 0.0)
            off = (s * cap) % count
            part += pltpu.roll(one, off, 1) if off else one
        select[:, b * count : (b + 1) * count] = part.astype(jnp.bfloat16)
    codes[...] = map_in[...].astype(jnp.int32)

    def wait_mag(s):
        def act():
            pltpu.make_async_remote_copy(
                src_ref=mags.at[s], dst_ref=mags.at[s], send_sem=mag_send.at[0], recv_sem=mag_recv.at[s],
                device_id=(me_l, me_s, me_r), device_id_type=MESH,
            ).wait_recv()

        pl.when((me_s > 0) | (me_own != s))(act)

    each(n_own, wait_mag)

    blon = whole(lambda o: mags[o, 0])
    blat = whole(lambda o: mags[o, 1])
    source = scale * (lon_up(blat) - lon_down(blat) - (lat_up(blon) - lat_down(blon)))
    phi = source
    for _ in range(SWEEPS - 1):
        phi = (
            ((1.0 - RELAX) * phi + source)
            + (east * lon_up(phi) + west * lon_down(phi))
            + (north * lat_up(phi) + south * lat_down(phi))
        )
    for i in range(n_lon):
        for j in range(n_rad):
            phis[i * n_rad + j] = phi[i * lons : (i + 1) * lons, j * lats : (j + 1) * lats]
    out_phi[...] = phis[me_own]

    points = fmap.shape[1]

    def look_up(s):
        patch = phis[s]
        for c in range(0, points, lats):
            code = codes[s, :, c : c + lats]
            low, high = code % lats, code // lats
            value = jnp.zeros((cap, lats), jnp.float32)
            for l in range(lons):
                line = jnp.broadcast_to(patch[l : l + 1, :], (cap, lats))
                found = jnp.take_along_axis(line, low, axis=1, mode="promise_in_bounds")
                value = jnp.where(high == l, found, value)
            recs[s, :, c : c + lats] = value

    each(n_own, look_up)
    rec = recs[...].reshape(n_own * cap, points)
    first = rec.astype(jnp.bfloat16)
    rest = rec - first.astype(jnp.float32)
    second = rest.astype(jnp.bfloat16)
    third = (rest - second.astype(jnp.float32)).astype(jnp.bfloat16)
    chosen = select[...]
    out_table[...] = (
        jnp.dot(chosen, first, preferred_element_type=jnp.float32)
        + jnp.dot(chosen, second, preferred_element_type=jnp.float32)
        + jnp.dot(chosen, third, preferred_element_type=jnp.float32)
    )

    for p in range(PHASES):
        for g in range(len(GROUPS)):
            for way in range(6):
                guarded(sends[way], lambda: halo(p, g, way).wait_send())

    def sent_mates(t, c):
        cond_copy(t).wait_send()
        row_copy(t).wait_send()
        map_copy(t).wait_send()
        return c

    lax.fori_loop(1, n_own, sent_mates, 0)

    @pl.when(me_s == 0)
    def _():
        def sent_mag(t, c):
            mag_copy(t).wait_send()
            return c

        lax.fori_loop(1, n_all, sent_mag, 0)


def shards(plasma_fields, velocity, resistivity, conductance, foot_map, foot_owner, foot_row):
    n_lon, n_sec, n_rad = lax.axis_size("lon"), lax.axis_size("sec"), lax.axis_size("rad")
    n_fields, shells, lons, lats = plasma_fields.shape
    count, points = foot_map.shape
    n_own, n_all, n_groups = n_lon * n_rad, n_lon * n_sec * n_rad, len(GROUPS)
    cap = max(8, 2 * count // n_own)
    sizes = (n_lon, n_sec, n_rad, n_fields, shells, lons, lats, cap)
    f32 = jnp.float32
    dma = pltpu.SemaphoreType.DMA
    vmem = pl.BlockSpec(memory_space=pltpu.VMEM)
    current, potential, table = pl.pallas_call(
        functools.partial(kernel, sizes),
        out_shape=(
            jax.ShapeDtypeStruct((n_fields, shells * lons, lats), f32),
            jax.ShapeDtypeStruct((lons, lats), f32),
            jax.ShapeDtypeStruct((ROWS_OWN, points), f32),
        ),
        in_specs=[vmem] * 7,
        out_specs=(vmem,) * 3,
        scratch_shapes=[
            pltpu.VMEM((4, shells * lons, lats), f32),
            pltpu.VMEM((7, lons, shells, lats), f32),
            pltpu.VMEM((PHASES, n_fields, lons + 2, shells, lats), f32),
            pltpu.VMEM((PHASES, 2, n_fields, lons, 1, lats), f32),
            pltpu.VMEM((PHASES, 2, n_fields, lons, 1, lats), f32),
            pltpu.VMEM((PHASES, n_groups, 2, shells, lats), f32),
            pltpu.VMEM((PHASES, n_groups, 2, shells, lats), f32),
            pltpu.VMEM((n_own, 2, lons, lats), f32),
            pltpu.VMEM((n_own, lons, lats), f32),
            pltpu.VMEM((n_own, cap, points), f32),
            pltpu.VMEM((n_own, cap, points), f32),
            pltpu.VMEM((n_own, 8, count), f32),
            pltpu.VMEM((n_own, 8, count), f32),
            pltpu.VMEM((n_own, lons, lats), f32),
            pltpu.VMEM((n_own, cap, points), f32),
            pltpu.VMEM((n_own, cap, points), jnp.int32),
            pltpu.VMEM((ROWS_OWN, n_own * cap), jnp.bfloat16),
            dma((PHASES, n_groups, 6)),
            dma((PHASES, n_groups, 6)),
            dma((n_all,)),
            dma((n_own,)),
            dma((n_own,)),
            dma((n_own,)),
            dma((n_own,)),
            dma((n_own,)),
            dma((n_own,)),
            dma((n_own,)),
        ],
        compiler_params=pltpu.CompilerParams(
            collective_id=0, has_side_effects=True, vmem_limit_bytes=48 * 1024 * 1024
        ),
    )(
        plasma_fields.reshape(n_fields, shells * lons, lats),
        velocity.reshape(3, shells * lons, lats),
        resistivity.reshape(shells * lons, lats),
        conductance,
        foot_map,
        foot_owner,
        foot_row.reshape(1, count),
    )
    return current.reshape(plasma_fields.shape), potential, table


def solution(mesh):
    in_specs = (
        P(None, "sec", "lon", "rad"),
        P(None, "sec", "lon", "rad"),
        P("sec", "lon", "rad"),
        P("lon", "rad"),
        P(("lon", "sec", "rad"), None),
        P(("lon", "sec", "rad"), None),
        P(("lon", "sec", "rad")),
    )
    out_specs = (P(None, "sec", "lon", "rad"), P("lon", "rad"), P(("lon", "sec", "rad"), None))
    return jax.shard_map(shards, mesh=mesh, in_specs=in_specs, out_specs=out_specs, check_vma=False)
```

```python
import functools

import jax
import jax.numpy as jnp
from jax import lax
from jax.experimental import pallas as pl
from jax.experimental.pallas import tpu as pltpu
from jax.sharding import PartitionSpec as P

PHASES = 4
SWEEPS = 8
ROWS_OWN = 32
COURANT = 0.25
DAMPING = 0.05
RELAX = 0.8
MESH = pl.DeviceIdType.MESH
ORDER = (5, 6, 0, 1, 2, 3, 4, 7)
GROUPS = ((0, 2), (2, 5), (5, 8))


def each(count, body):
    if count <= 16:
        for i in range(count):
            body(i)
    else:
        lax.fori_loop(0, count, lambda i, c: (body(i), c)[1], 0)


def kernel(
    sizes,
    fields_at, vel_at, res_at, cond_at, fmap_at, fowner_at, frow_at,
    end_fields, end_phi, end_table,
    out, out_phi, out_table, store_sem, fields, vel, res, cond, fmap, fowner, frow, load_sem,
    wide, coef, cells, shell_out, shell_in, lat_out, lat_in,
    mags, map_out, map_in, side_out, side_in, phis, recs, codes, select,
    halo_send, halo_recv, mag_send, mag_recv, map_send, map_recv, side_send, side_recv,
):
    n_lon, n_sec, n_rad, n_fields, shells, lons, lats, cap = sizes
    me_l, me_s, me_r = lax.axis_index("lon"), lax.axis_index("sec"), lax.axis_index("rad")
    n_all, n_own = n_lon * n_sec * n_rad, n_lon * n_rad
    me_own = me_l * n_rad + me_r
    me_flat = (me_l * n_sec + me_s) * n_rad + me_r

    loads = [
        pltpu.make_async_copy(src, dst, load_sem.at[i])
        for i, (src, dst) in enumerate(
            (
                (fields_at, fields), (vel_at, vel), (res_at, res), (cond_at, cond),
                (fmap_at, fmap), (fowner_at, fowner), (frow_at, frow),
            )
        )
    ]
    for load in loads:
        load.start()

    def turn(me, by, count):
        return lax.rem(me + by, count)

    def peer(t):
        dl, ds, dr = t // (n_sec * n_rad), (t // n_rad) % n_sec, t % n_rad
        return (turn(me_l, dl, n_lon), turn(me_s, ds, n_sec), turn(me_r, dr, n_rad))

    def mate(t):
        return (turn(me_l, t // n_rad, n_lon), me_s, turn(me_r, t % n_rad, n_rad))

    def others(count, body):
        if count <= 64:
            for t in range(1, count):
                body(t)
        else:
            lax.fori_loop(1, count, lambda t, c: (body(t), c)[1], 0)

    barrier = pltpu.get_barrier_semaphore()
    others(n_all, lambda t: pl.semaphore_signal(barrier, inc=1, device_id=peer(t), device_id_type=MESH))

    lane = lax.broadcasted_iota(jnp.int32, (shells, lats), 1)
    lane3 = lax.broadcasted_iota(jnp.int32, (lons, shells, lats), 2)
    row3 = lax.broadcasted_iota(jnp.int32, (lons, shells, lats), 1)

    def publish(p, g, blocks):
        f0, _ = GROUPS[g]
        low = jnp.zeros((shells, lats), jnp.float32)
        high = jnp.zeros((shells, lats), jnp.float32)
        for i, block in enumerate(blocks):
            f = f0 + i
            cells[p, f, 1 : lons + 1] = block
            shell_out[p, 0, f] = block[:, 0:1, :]
            shell_out[p, 1, f] = block[:, shells - 1 : shells, :]
            for l in range(lons):
                k = i * lons + l
                low = jnp.where(lane == k, pltpu.roll(block[l], k, 1) if k else block[l], low)
                high = jnp.where(lane == k, pltpu.roll(block[l], k + 1, 1), high)
        lat_out[p, g, 0] = low
        lat_out[p, g, 1] = high

    left, right = lax.rem(me_l + n_lon - 1, n_lon), lax.rem(me_l + 1, n_lon)

    def halo(p, g, way):
        f0, f1 = GROUPS[g]
        span = pl.ds(f0, f1 - f0)
        src, dst, to = (
            (lambda: (cells.at[p, span, 1], cells.at[p, span, lons + 1], (left, me_s, me_r))),
            (lambda: (cells.at[p, span, lons], cells.at[p, span, 0], (right, me_s, me_r))),
            (lambda: (shell_out.at[p, 0, span], shell_in.at[p, 1, span], (me_l, me_s - 1, me_r))),
            (lambda: (shell_out.at[p, 1, span], shell_in.at[p, 0, span], (me_l, me_s + 1, me_r))),
            (lambda: (lat_out.at[p, g, 0], lat_in.at[p, g, 1], (me_l, me_s, me_r - 1))),
            (lambda: (lat_out.at[p, g, 1], lat_in.at[p, g, 0], (me_l, me_s, me_r + 1))),
        )[way]()
        return pltpu.make_async_remote_copy(
            src_ref=src, dst_ref=dst, send_sem=halo_send.at[way], recv_sem=halo_recv.at[p, g, way],
            device_id=to, device_id_type=MESH,
        )

    sends = (None, None, me_s > 0, me_s < n_sec - 1, me_r > 0, me_r < n_rad - 1)
    takes = (None, None, me_s < n_sec - 1, me_s > 0, me_r < n_rad - 1, me_r > 0)

    def guarded(cond_value, act):
        if cond_value is None:
            act()
        else:
            pl.when(cond_value)(act)

    def start_halo(p, g):
        for way in (0, 1, 4, 5, 2, 3):
            guarded(sends[way], lambda: halo(p, g, way).start())

    def wait_halo(p, g):
        for way in range(6):
            guarded(takes[way], lambda: halo(p, g, way).wait_recv())

    loads[0].wait()
    for g, (f0, f1) in enumerate(GROUPS):
        blocks = []
        for f in ORDER[f0:f1]:
            blocks.append(jnp.stack([fields[f, pl.ds(l, shells, stride=lons), :] for l in range(lons)]))
        publish(0, g, blocks)

    @pl.when(me_s == 0)
    def _():
        shell_in[:, 0] = jnp.zeros_like(shell_in[:, 0])

    @pl.when(me_s == n_sec - 1)
    def _():
        shell_in[:, 1] = jnp.zeros_like(shell_in[:, 1])

    @pl.when(me_r == 0)
    def _():
        lat_in[:, :, 0] = jnp.zeros_like(lat_in[:, :, 0])

    @pl.when(me_r == n_rad - 1)
    def _():
        lat_in[:, :, 1] = jnp.zeros_like(lat_in[:, :, 1])

    pl.semaphore_wait(barrier, n_all - 1)

    for g in range(len(GROUPS)):
        start_halo(0, g)

    loads[1].wait()
    loads[2].wait()
    wide[0:3] = vel[...].astype(jnp.float32)
    wide[3] = res[...].astype(jnp.float32)
    for l in range(lons):
        w = [wide[d, pl.ds(l, shells, stride=lons), :] for d in range(3)]
        r = wide[3, pl.ds(l, shells, stride=lons), :]
        middle = 1.0 - 6.0 * r
        for d in range(3):
            up = COURANT * jnp.maximum(w[d], 0.0)
            down = COURANT * jnp.minimum(w[d], 0.0)
            coef[1 + 2 * d, l] = r + up
            coef[2 + 2 * d, l] = r - down
            middle = middle - (up - down)
        coef[0, l] = middle

    def step(p, g, i):
        f = GROUPS[g][0] + i
        here = cells[p, f, 1 : lons + 1]
        total = coef[0] * here
        total += coef[3] * cells[p, f, 0:lons] + coef[4] * cells[p, f, 2 : lons + 2]
        lower = jnp.where(row3 == 0, shell_in[p, 0, f], pltpu.roll(here, 1, 1))
        upper = jnp.where(row3 == shells - 1, shell_in[p, 1, f], pltpu.roll(here, shells - 1, 1))
        total += coef[1] * lower + coef[2] * upper
        low_edge, high_edge = lat_in[p, g, 0], lat_in[p, g, 1]
        ks = [i * lons + l for l in range(lons)]
        low_edges = jnp.stack([pltpu.roll(low_edge, lats - k, 1) if k else low_edge for k in ks])
        high_edges = jnp.stack([pltpu.roll(high_edge, lats - 1 - k, 1) for k in ks])
        lower = jnp.where(lane3 == 0, low_edges, pltpu.roll(here, 1, 2))
        upper = jnp.where(lane3 == lats - 1, high_edges, pltpu.roll(here, lats - 1, 2))
        return total + coef[5] * lower + coef[6] * upper

    def mag_copy(t):
        return pltpu.make_async_remote_copy(
            src_ref=mags.at[me_own], dst_ref=mags.at[me_own], send_sem=mag_send,
            recv_sem=mag_recv.at[me_own], device_id=peer(t), device_id_type=MESH,
        )

    for p in range(PHASES):
        if p == 1:
            for load in loads[3:]:
                load.wait()
            count, points = fmap.shape
            g_row = lax.broadcasted_iota(jnp.int32, (count, count), 0)
            g_lane = lax.broadcasted_iota(jnp.int32, (count, count), 1)
            owner_l = jnp.broadcast_to(fowner[...].astype(jnp.float32), (count, count))
            row_l = jnp.broadcast_to(frow[...].astype(jnp.float32), (count, count))
            same = g_row == g_lane
            owner_c = jnp.sum(jnp.where(same, owner_l, 0.0), axis=1, keepdims=True)
            row_c = jnp.sum(jnp.where(same, row_l, 0.0), axis=1, keepdims=True)
            alike = owner_c == owner_l
            rank_l = jnp.sum(jnp.where(alike & (g_row < g_lane), 1.0, 0.0), axis=0, keepdims=True)
            rank_c = jnp.sum(jnp.where(alike & (g_row > g_lane), 1.0, 0.0), axis=1, keepdims=True)
            key_l = owner_l[0:1] * float(cap) + rank_l
            key_c = owner_c * float(count) + rank_c
            spot = lax.broadcasted_iota(jnp.int32, (n_own * cap, count), 0).astype(jnp.float32)
            spot_l = g_lane.astype(jnp.float32)
            ids = fmap[...]
            high_part = (ids // lats).astype(jnp.float32).astype(jnp.bfloat16)
            low_part = (ids % lats).astype(jnp.float32).astype(jnp.bfloat16)
            pick = jnp.where(spot == key_l, 1.0, 0.0).astype(jnp.bfloat16)
            highs = jnp.dot(pick, high_part, preferred_element_type=jnp.float32)
            lows = jnp.dot(pick, low_part, preferred_element_type=jnp.float32)
            map_out[...] = (highs * float(lats) + lows).reshape(n_own, cap, points)

            def side_owner(o):
                base = jnp.asarray(o * count, jnp.int32).astype(jnp.float32)
                hit = spot_l + base == key_c
                rows = jnp.sum(jnp.where(hit, row_c + 1.0, 0.0), axis=0, keepdims=True) - 1.0
                side_out[o, 0:8] = jnp.broadcast_to(rows, (8, count))
                side_out[o, 8 : 8 + lons] = cond[...]

            each(n_own, side_owner)
            map_in[me_own] = map_out[me_own]
            side_in[me_own] = side_out[me_own]

            def to_mate(t, src, dst, send, recv):
                l, _, r = mate(t)
                return pltpu.make_async_remote_copy(
                    src_ref=src.at[l * n_rad + r], dst_ref=dst.at[me_own], send_sem=send, recv_sem=recv.at[t],
                    device_id=(l, me_s, r), device_id_type=MESH,
                )

            def map_copy(t):
                return to_mate(t, map_out, map_in, map_send, map_recv)

            def side_copy(t):
                return to_mate(t, side_out, side_in, side_send, side_recv)

            def start_mate(t):
                side_copy(t).start()
                map_copy(t).start()

            others(n_own, start_mate)
        for g, (f0, f1) in enumerate(GROUPS):
            wait_halo(p, g)
            blocks = [step(p, g, i) for i in range(f1 - f0)]
            if p < PHASES - 1:
                publish(p + 1, g, blocks)
                start_halo(p + 1, g)
                continue
            if g == 0:

                @pl.when(me_s == 0)
                def _():
                    for c in range(2):
                        for l in range(lons):
                            mags[me_own, c, l : l + 1, :] = blocks[c][l, 0:1, :]

                    others(n_all, lambda t: mag_copy(t).start())

            for i in range(f1 - f0):
                for l in range(lons):
                    out[ORDER[f0 + i], pl.ds(l, shells, stride=lons), :] = blocks[i][l]

    stores = [
        pltpu.make_async_copy(src, dst, store_sem.at[i])
        for i, (src, dst) in enumerate(((out, end_fields), (out_phi, end_phi), (out_table, end_table)))
    ]
    stores[0].start()

    def wait_mate(t):
        side_copy(t).wait_recv()
        map_copy(t).wait_recv()

    others(n_own, wait_mate)

    def whole(get):
        return jnp.concatenate(
            [jnp.concatenate([get(i * n_rad + j) for j in range(n_rad)], axis=1) for i in range(n_lon)], axis=0
        )

    nl, nt = n_lon * lons, n_rad * lats
    t_full = lax.broadcasted_iota(jnp.int32, (nl, nt), 1)

    def lon_up(x):
        return pltpu.roll(x, nl - 1, 0)

    def lon_down(x):
        return pltpu.roll(x, 1, 0)

    def lat_up(x):
        return jnp.where(t_full == nt - 1, 0.0, pltpu.roll(x, nt - 1, 1))

    def lat_down(x):
        return jnp.where(t_full == 0, 0.0, pltpu.roll(x, 1, 1))

    c_full = whole(lambda o: side_in[o, 8 : 8 + lons])
    east = 0.5 * (c_full + lon_up(c_full))
    west = 0.5 * (c_full + lon_down(c_full))
    north = 0.5 * (c_full + lat_up(c_full))
    south = 0.5 * (c_full + lat_down(c_full))
    scale = RELAX / (DAMPING * c_full + east + west + north + south)
    east, west, north, south = east * scale, west * scale, north * scale, south * scale

    rows_at = lax.broadcasted_iota(jnp.int32, (ROWS_OWN, count), 0).astype(jnp.float32)
    per = count // cap
    for b in range(n_own // per if n_own >= per else 1):
        part = jnp.zeros((ROWS_OWN, count), jnp.float32)
        for s in range(b * per, min((b + 1) * per, n_own)):
            one = jnp.where(rows_at == side_in[s, 0:1, :], 1.0, 0.0)
            off = (s * cap) % count
            part += pltpu.roll(one, off, 1) if off else one
        select[:, b * count : (b + 1) * count] = part.astype(jnp.bfloat16)
    codes[...] = map_in[...].astype(jnp.int32)

    def wait_mag(s):
        def act():
            pltpu.make_async_remote_copy(
                src_ref=mags.at[s], dst_ref=mags.at[s], send_sem=mag_send, recv_sem=mag_recv.at[s],
                device_id=(me_l, me_s, me_r), device_id_type=MESH,
            ).wait_recv()

        pl.when((me_s > 0) | (me_own != s))(act)

    each(n_own, wait_mag)

    blon = whole(lambda o: mags[o, 0])
    blat = whole(lambda o: mags[o, 1])
    source = scale * (lon_up(blat) - lon_down(blat) - (lat_up(blon) - lat_down(blon)))
    phi = source
    for _ in range(SWEEPS - 1):
        phi = (
            ((1.0 - RELAX) * phi + source)
            + (east * lon_up(phi) + west * lon_down(phi))
            + (north * lat_up(phi) + south * lat_down(phi))
        )
    for i in range(n_lon):
        for j in range(n_rad):
            phis[i * n_rad + j] = phi[i * lons : (i + 1) * lons, j * lats : (j + 1) * lats]
    out_phi[...] = phis[me_own]
    stores[1].start()

    def look_up(s):
        patch = phis[s]
        for c in range(0, points, lats):
            code = codes[s, :, c : c + lats]
            low, high = code % lats, code // lats
            value = jnp.zeros((cap, lats), jnp.float32)
            for l in range(lons):
                line = jnp.broadcast_to(patch[l : l + 1, :], (cap, lats))
                found = jnp.take_along_axis(line, low, axis=1, mode="promise_in_bounds")
                value = jnp.where(high == l, found, value)
            recs[s, :, c : c + lats] = value

    each(n_own, look_up)
    rec = recs[...].reshape(n_own * cap, points)
    first = rec.astype(jnp.bfloat16)
    rest = rec - first.astype(jnp.float32)
    second = rest.astype(jnp.bfloat16)
    third = (rest - second.astype(jnp.float32)).astype(jnp.bfloat16)
    chosen = select[...]
    out_table[...] = (
        jnp.dot(chosen, first, preferred_element_type=jnp.float32)
        + jnp.dot(chosen, second, preferred_element_type=jnp.float32)
        + jnp.dot(chosen, third, preferred_element_type=jnp.float32)
    )

    stores[2].start()

    def sent(ref, sem):
        pltpu.make_async_copy(ref, ref, sem).wait()

    for way, ref in enumerate(
        (
            cells.at[:, :, 1], cells.at[:, :, lons],
            shell_out.at[:, 0], shell_out.at[:, 1], lat_out.at[:, :, 0], lat_out.at[:, :, 1],
        )
    ):
        guarded(sends[way], lambda: sent(ref, halo_send.at[way]))
    sent(map_out.at[1:n_own], map_send)
    sent(side_out.at[1:n_own], side_send)

    @pl.when(me_s == 0)
    def _():
        for first in range(1, n_all, n_own):
            last = min(first + n_own, n_all)
            sent(mags.at[0 : last - first], mag_send)

    for store in stores:
        store.wait()


def write_out(fields, phi, table, out, out_phi, out_table, sems):
    copies = [
        pltpu.make_async_copy(src, dst, sems.at[i])
        for i, (src, dst) in enumerate(((fields, out), (phi, out_phi), (table, out_table)))
    ]
    for copy in copies:
        copy.start()
    for copy in copies:
        copy.wait()


def shards(plasma_fields, velocity, resistivity, conductance, foot_map, foot_owner, foot_row):
    n_lon, n_sec, n_rad = lax.axis_size("lon"), lax.axis_size("sec"), lax.axis_size("rad")
    n_fields, shells, lons, lats = plasma_fields.shape
    count, points = foot_map.shape
    n_own, n_all, n_groups = n_lon * n_rad, n_lon * n_sec * n_rad, len(GROUPS)
    cap = max(8, 2 * count // n_own)
    sizes = (n_lon, n_sec, n_rad, n_fields, shells, lons, lats, cap)
    f32 = jnp.float32
    dma = pltpu.SemaphoreType.DMA
    hbm = pl.BlockSpec(memory_space=pltpu.HBM)
    results = (
        jax.ShapeDtypeStruct((n_fields, shells * lons, lats), f32),
        jax.ShapeDtypeStruct((lons, lats), f32),
        jax.ShapeDtypeStruct((ROWS_OWN, points), f32),
    )
    made = pl.pallas_call(
        functools.partial(kernel, sizes),
        out_shape=results,
        in_specs=[hbm] * 7,
        out_specs=(hbm,) * 3,
        scratch_shapes=[
            pltpu.VMEM((n_fields, shells * lons, lats), f32),
            pltpu.VMEM((lons, lats), f32),
            pltpu.VMEM((ROWS_OWN, points), f32),
            dma((3,)),
            pltpu.VMEM((n_fields, shells * lons, lats), f32),
            pltpu.VMEM((3, shells * lons, lats), velocity.dtype),
            pltpu.VMEM((shells * lons, lats), resistivity.dtype),
            pltpu.VMEM((lons, lats), f32),
            pltpu.VMEM((count, points), jnp.int32),
            pltpu.VMEM((1, count), jnp.int32),
            pltpu.VMEM((1, count), jnp.int32),
            dma((7,)),
            pltpu.VMEM((4, shells * lons, lats), f32),
            pltpu.VMEM((7, lons, shells, lats), f32),
            pltpu.VMEM((PHASES, n_fields, lons + 2, shells, lats), f32),
            pltpu.VMEM((PHASES, 2, n_fields, lons, 1, lats), f32),
            pltpu.VMEM((PHASES, 2, n_fields, lons, 1, lats), f32),
            pltpu.VMEM((PHASES, n_groups, 2, shells, lats), f32),
            pltpu.VMEM((PHASES, n_groups, 2, shells, lats), f32),
            pltpu.VMEM((n_own, 2, lons, lats), f32),
            pltpu.VMEM((n_own, cap, points), f32),
            pltpu.VMEM((n_own, cap, points), f32),
            pltpu.VMEM((n_own, 8 + lons, count), f32),
            pltpu.VMEM((n_own, 8 + lons, count), f32),
            pltpu.VMEM((n_own, lons, lats), f32),
            pltpu.VMEM((n_own, cap, points), f32),
            pltpu.VMEM((n_own, cap, points), jnp.int32),
            pltpu.VMEM((ROWS_OWN, n_own * cap), jnp.bfloat16),
            dma((6,)),
            dma((PHASES, n_groups, 6)),
            dma,
            dma((n_own,)),
            dma,
            dma((n_own,)),
            dma,
            dma((n_own,)),
        ],
        compiler_params=pltpu.CompilerParams(
            collective_id=0, has_side_effects=True, vmem_limit_bytes=64 * 1024 * 1024
        ),
    )(
        plasma_fields.reshape(n_fields, shells * lons, lats),
        velocity.reshape(3, shells * lons, lats),
        resistivity.reshape(shells * lons, lats),
        conductance,
        foot_map,
        foot_owner.reshape(1, count),
        foot_row.reshape(1, count),
    )
    current, potential, table = pl.pallas_call(
        write_out,
        out_shape=results,
        in_specs=[hbm] * 3,
        out_specs=(hbm,) * 3,
        scratch_shapes=[dma((3,))],
        compiler_params=pltpu.CompilerParams(vmem_limit_bytes=64 * 1024 * 1024),
    )(*made)
    return current.reshape(plasma_fields.shape), potential, table


def solution(mesh):
    in_specs = (
        P(None, "sec", "lon", "rad"),
        P(None, "sec", "lon", "rad"),
        P("sec", "lon", "rad"),
        P("lon", "rad"),
        P(("lon", "sec", "rad"), None),
        P(("lon", "sec", "rad"), None),
        P(("lon", "sec", "rad")),
    )
    out_specs = (P(None, "sec", "lon", "rad"), P("lon", "rad"), P(("lon", "sec", "rad"), None))
    return jax.shard_map(shards, mesh=mesh, in_specs=in_specs, out_specs=out_specs, check_vma=False)
```

```python
import functools

import jax
import jax.numpy as jnp
from jax import lax
from jax.experimental import pallas as pl
from jax.experimental.pallas import tpu as pltpu
from jax.sharding import PartitionSpec as P

PHASES = 4
SWEEPS = 8
ROWS_OWN = 32
COURANT = 0.25
DAMPING = 0.05
RELAX = 0.8
MESH = pl.DeviceIdType.MESH
ORDER = (5, 6, 0, 1, 2, 3, 4, 7)
GROUPS = ((0, 2), (2, 5), (5, 8))


def each(count, body):
    if count <= 16:
        for i in range(count):
            body(i)
    else:
        lax.fori_loop(0, count, lambda i, c: (body(i), c)[1], 0)


def kernel(
    sizes,
    fields_at, vel_at, res_at, cond_at, fmap_at, fowner_at, frow_at,
    end_fields, end_phi, end_table,
    out, out_phi, out_table, store_sem, fields, vel, res, cond, fmap, fowner, frow, load_sem,
    wide, coef, cells, shell_out, shell_in, lat_out, lat_in,
    mags, map_out, map_in, side_out, side_in, phis, recs, codes, select,
    halo_send, halo_recv, mag_send, mag_recv, map_send, map_recv, side_send, side_recv,
):
    n_lon, n_sec, n_rad, n_fields, shells, lons, lats, cap = sizes
    me_l, me_s, me_r = lax.axis_index("lon"), lax.axis_index("sec"), lax.axis_index("rad")
    n_all, n_own = n_lon * n_sec * n_rad, n_lon * n_rad
    me_own = me_l * n_rad + me_r
    me_flat = (me_l * n_sec + me_s) * n_rad + me_r

    loads = [
        pltpu.make_async_copy(src, dst, load_sem.at[i])
        for i, (src, dst) in enumerate(
            (
                (fields_at, fields), (vel_at, vel), (res_at, res), (cond_at, cond),
                (fmap_at, fmap), (fowner_at, fowner), (frow_at, frow),
            )
        )
    ]
    for load in loads:
        load.start()

    def turn(me, by, count):
        return lax.rem(me + by, count)

    def peer(t):
        dl, ds, dr = t // (n_sec * n_rad), (t // n_rad) % n_sec, t % n_rad
        return (turn(me_l, dl, n_lon), turn(me_s, ds, n_sec), turn(me_r, dr, n_rad))

    def mate(t):
        return (turn(me_l, t // n_rad, n_lon), me_s, turn(me_r, t % n_rad, n_rad))

    def others(count, body):
        if count <= 64:
            for t in range(1, count):
                body(t)
        else:
            lax.fori_loop(1, count, lambda t, c: (body(t), c)[1], 0)

    barrier = pltpu.get_barrier_semaphore()
    others(n_all, lambda t: pl.semaphore_signal(barrier, inc=1, device_id=peer(t), device_id_type=MESH))

    lane = lax.broadcasted_iota(jnp.int32, (shells, lats), 1)
    lane3 = lax.broadcasted_iota(jnp.int32, (lons, shells, lats), 2)
    row3 = lax.broadcasted_iota(jnp.int32, (lons, shells, lats), 1)

    def publish(p, g, blocks):
        f0, _ = GROUPS[g]
        low = jnp.zeros((shells, lats), jnp.float32)
        high = jnp.zeros((shells, lats), jnp.float32)
        for i, block in enumerate(blocks):
            f = f0 + i
            cells[p, f, 1 : lons + 1] = block
            shell_out[p, 0, f] = block[:, 0:1, :]
            shell_out[p, 1, f] = block[:, shells - 1 : shells, :]
            for l in range(lons):
                k = i * lons + l
                low = jnp.where(lane == k, pltpu.roll(block[l], k, 1) if k else block[l], low)
                high = jnp.where(lane == k, pltpu.roll(block[l], k + 1, 1), high)
        lat_out[p, g, 0] = low
        lat_out[p, g, 1] = high

    left, right = lax.rem(me_l + n_lon - 1, n_lon), lax.rem(me_l + 1, n_lon)

    def halo(p, g, way):
        f0, f1 = GROUPS[g]
        span = pl.ds(f0, f1 - f0)
        src, dst, to = (
            (lambda: (cells.at[p, span, 1], cells.at[p, span, lons + 1], (left, me_s, me_r))),
            (lambda: (cells.at[p, span, lons], cells.at[p, span, 0], (right, me_s, me_r))),
            (lambda: (shell_out.at[p, 0, span], shell_in.at[p, 1, span], (me_l, me_s - 1, me_r))),
            (lambda: (shell_out.at[p, 1, span], shell_in.at[p, 0, span], (me_l, me_s + 1, me_r))),
            (lambda: (lat_out.at[p, g, 0], lat_in.at[p, g, 1], (me_l, me_s, me_r - 1))),
            (lambda: (lat_out.at[p, g, 1], lat_in.at[p, g, 0], (me_l, me_s, me_r + 1))),
        )[way]()
        return pltpu.make_async_remote_copy(
            src_ref=src, dst_ref=dst, send_sem=halo_send.at[way], recv_sem=halo_recv.at[p, g, way],
            device_id=to, device_id_type=MESH,
        )

    sends = (None, None, me_s > 0, me_s < n_sec - 1, me_r > 0, me_r < n_rad - 1)
    takes = (None, None, me_s < n_sec - 1, me_s > 0, me_r < n_rad - 1, me_r > 0)

    def guarded(cond_value, act):
        if cond_value is None:
            act()
        else:
            pl.when(cond_value)(act)

    def start_halo(p, g):
        for way in (4, 5, 2, 3, 0, 1):
            guarded(sends[way], lambda: halo(p, g, way).start())

    def wait_halo(p, g):
        for way in range(6):
            guarded(takes[way], lambda: halo(p, g, way).wait_recv())

    loads[0].wait()
    for g, (f0, f1) in enumerate(GROUPS):
        blocks = []
        for f in ORDER[f0:f1]:
            blocks.append(jnp.stack([fields[f, pl.ds(l, shells, stride=lons), :] for l in range(lons)]))
        publish(0, g, blocks)

    @pl.when(me_s == 0)
    def _():
        shell_in[:, 0] = jnp.zeros_like(shell_in[:, 0])

    @pl.when(me_s == n_sec - 1)
    def _():
        shell_in[:, 1] = jnp.zeros_like(shell_in[:, 1])

    @pl.when(me_r == 0)
    def _():
        lat_in[:, :, 0] = jnp.zeros_like(lat_in[:, :, 0])

    @pl.when(me_r == n_rad - 1)
    def _():
        lat_in[:, :, 1] = jnp.zeros_like(lat_in[:, :, 1])

    pl.semaphore_wait(barrier, n_all - 1)

    for g in range(len(GROUPS)):
        start_halo(0, g)

    for load in loads[3:]:
        load.wait()
    count, points = fmap.shape
    g_row = lax.broadcasted_iota(jnp.int32, (count, count), 0)
    g_lane = lax.broadcasted_iota(jnp.int32, (count, count), 1)
    owner_l = jnp.broadcast_to(fowner[...].astype(jnp.float32), (count, count))
    row_l = jnp.broadcast_to(frow[...].astype(jnp.float32), (count, count))
    same = g_row == g_lane
    owner_c = jnp.sum(jnp.where(same, owner_l, 0.0), axis=1, keepdims=True)
    row_c = jnp.sum(jnp.where(same, row_l, 0.0), axis=1, keepdims=True)
    alike = owner_c == owner_l
    rank_l = jnp.sum(jnp.where(alike & (g_row < g_lane), 1.0, 0.0), axis=0, keepdims=True)
    rank_c = jnp.sum(jnp.where(alike & (g_row > g_lane), 1.0, 0.0), axis=1, keepdims=True)
    key_l = owner_l[0:1] * float(cap) + rank_l
    key_c = owner_c * float(count) + rank_c
    spot = lax.broadcasted_iota(jnp.int32, (n_own * cap, count), 0).astype(jnp.float32)
    spot_l = g_lane.astype(jnp.float32)
    ids = fmap[...]
    high_part = (ids // lats).astype(jnp.float32).astype(jnp.bfloat16)
    low_part = (ids % lats).astype(jnp.float32).astype(jnp.bfloat16)
    pick = jnp.where(spot == key_l, 1.0, 0.0).astype(jnp.bfloat16)
    highs = jnp.dot(pick, high_part, preferred_element_type=jnp.float32)
    lows = jnp.dot(pick, low_part, preferred_element_type=jnp.float32)
    map_out[...] = (highs * float(lats) + lows).reshape(n_own, cap, points)

    def side_owner(o):
        base = jnp.asarray(o * count, jnp.int32).astype(jnp.float32)
        hit = spot_l + base == key_c
        rows = jnp.sum(jnp.where(hit, row_c + 1.0, 0.0), axis=0, keepdims=True) - 1.0
        side_out[o, 0:8] = jnp.broadcast_to(rows, (8, count))
        side_out[o, 8 : 8 + lons] = cond[...]

    each(n_own, side_owner)
    map_in[me_own] = map_out[me_own]
    side_in[me_own] = side_out[me_own]

    def to_mate(t, src, dst, send, recv):
        l, _, r = mate(t)
        return pltpu.make_async_remote_copy(
            src_ref=src.at[l * n_rad + r], dst_ref=dst.at[me_own], send_sem=send, recv_sem=recv.at[t],
            device_id=(l, me_s, r), device_id_type=MESH,
        )

    def map_copy(t):
        return to_mate(t, map_out, map_in, map_send, map_recv)

    def side_copy(t):
        return to_mate(t, side_out, side_in, side_send, side_recv)

    def start_mate(t):
        side_copy(t).start()
        map_copy(t).start()

    if n_own > 64:
        others(n_own, start_mate)

    loads[1].wait()
    loads[2].wait()
    wide[0:3] = vel[...].astype(jnp.float32)
    wide[3] = res[...].astype(jnp.float32)
    for l in range(lons):
        w = [wide[d, pl.ds(l, shells, stride=lons), :] for d in range(3)]
        r = wide[3, pl.ds(l, shells, stride=lons), :]
        middle = 1.0 - 6.0 * r
        for d in range(3):
            up = COURANT * jnp.maximum(w[d], 0.0)
            down = COURANT * jnp.minimum(w[d], 0.0)
            coef[1 + 2 * d, l] = r + up
            coef[2 + 2 * d, l] = r - down
            middle = middle - (up - down)
        coef[0, l] = middle

    def step(p, g, i):
        f = GROUPS[g][0] + i
        here = cells[p, f, 1 : lons + 1]
        total = coef[0] * here
        total += coef[3] * cells[p, f, 0:lons] + coef[4] * cells[p, f, 2 : lons + 2]
        lower = jnp.where(row3 == 0, shell_in[p, 0, f], pltpu.roll(here, 1, 1))
        upper = jnp.where(row3 == shells - 1, shell_in[p, 1, f], pltpu.roll(here, shells - 1, 1))
        total += coef[1] * lower + coef[2] * upper
        low_edge, high_edge = lat_in[p, g, 0], lat_in[p, g, 1]
        ks = [i * lons + l for l in range(lons)]
        low_edges = jnp.stack([pltpu.roll(low_edge, lats - k, 1) if k else low_edge for k in ks])
        high_edges = jnp.stack([pltpu.roll(high_edge, lats - 1 - k, 1) for k in ks])
        lower = jnp.where(lane3 == 0, low_edges, pltpu.roll(here, 1, 2))
        upper = jnp.where(lane3 == lats - 1, high_edges, pltpu.roll(here, lats - 1, 2))
        return total + coef[5] * lower + coef[6] * upper

    def mag_copy(t):
        return pltpu.make_async_remote_copy(
            src_ref=mags.at[me_own], dst_ref=mags.at[me_own], send_sem=mag_send,
            recv_sem=mag_recv.at[me_own], device_id=peer(t), device_id_type=MESH,
        )

    for p in range(PHASES):
        for t in range(1 + p, n_own, PHASES) if n_own <= 64 else ():
            start_mate(t)
        for g, (f0, f1) in enumerate(GROUPS):
            wait_halo(p, g)
            blocks = [step(p, g, i) for i in range(f1 - f0)]
            if p < PHASES - 1:
                publish(p + 1, g, blocks)
                start_halo(p + 1, g)
                continue
            if g == 0:

                @pl.when(me_s == 0)
                def _():
                    for c in range(2):
                        for l in range(lons):
                            mags[me_own, c, l : l + 1, :] = blocks[c][l, 0:1, :]

                    others(n_all, lambda t: mag_copy(t).start())

            for i in range(f1 - f0):
                for l in range(lons):
                    out[ORDER[f0 + i], pl.ds(l, shells, stride=lons), :] = blocks[i][l]

    stores = [
        pltpu.make_async_copy(src, dst, store_sem.at[i])
        for i, (src, dst) in enumerate(((out, end_fields), (out_phi, end_phi), (out_table, end_table)))
    ]
    stores[0].start()

    def wait_mate(t):
        side_copy(t).wait_recv()
        map_copy(t).wait_recv()

    others(n_own, wait_mate)

    def whole(get):
        return jnp.concatenate(
            [jnp.concatenate([get(i * n_rad + j) for j in range(n_rad)], axis=1) for i in range(n_lon)], axis=0
        )

    nl, nt = n_lon * lons, n_rad * lats
    t_full = lax.broadcasted_iota(jnp.int32, (nl, nt), 1)

    def lon_up(x):
        return pltpu.roll(x, nl - 1, 0)

    def lon_down(x):
        return pltpu.roll(x, 1, 0)

    def lat_up(x):
        return jnp.where(t_full == nt - 1, 0.0, pltpu.roll(x, nt - 1, 1))

    def lat_down(x):
        return jnp.where(t_full == 0, 0.0, pltpu.roll(x, 1, 1))

    c_full = whole(lambda o: side_in[o, 8 : 8 + lons])
    east = 0.5 * (c_full + lon_up(c_full))
    west = 0.5 * (c_full + lon_down(c_full))
    north = 0.5 * (c_full + lat_up(c_full))
    south = 0.5 * (c_full + lat_down(c_full))
    scale = RELAX / (DAMPING * c_full + east + west + north + south)
    east, west, north, south = east * scale, west * scale, north * scale, south * scale

    rows_at = lax.broadcasted_iota(jnp.int32, (ROWS_OWN, count), 0).astype(jnp.float32)
    per = count // cap
    for b in range(n_own // per if n_own >= per else 1):
        part = jnp.zeros((ROWS_OWN, count), jnp.float32)
        for s in range(b * per, min((b + 1) * per, n_own)):
            one = jnp.where(rows_at == side_in[s, 0:1, :], 1.0, 0.0)
            off = (s * cap) % count
            part += pltpu.roll(one, off, 1) if off else one
        select[:, b * count : (b + 1) * count] = part.astype(jnp.bfloat16)
    codes[...] = map_in[...].astype(jnp.int32)

    def wait_mag(s):
        def act():
            pltpu.make_async_remote_copy(
                src_ref=mags.at[s], dst_ref=mags.at[s], send_sem=mag_send, recv_sem=mag_recv.at[s],
                device_id=(me_l, me_s, me_r), device_id_type=MESH,
            ).wait_recv()

        pl.when((me_s > 0) | (me_own != s))(act)

    each(n_own, wait_mag)

    blon = whole(lambda o: mags[o, 0])
    blat = whole(lambda o: mags[o, 1])
    source = scale * (lon_up(blat) - lon_down(blat) - (lat_up(blon) - lat_down(blon)))
    phi = source
    for _ in range(SWEEPS - 1):
        phi = (
            ((1.0 - RELAX) * phi + source)
            + (east * lon_up(phi) + west * lon_down(phi))
            + (north * lat_up(phi) + south * lat_down(phi))
        )
    for i in range(n_lon):
        for j in range(n_rad):
            phis[i * n_rad + j] = phi[i * lons : (i + 1) * lons, j * lats : (j + 1) * lats]
    out_phi[...] = phis[me_own]
    stores[1].start()

    def look_up(s):
        patch = phis[s]
        for c in range(0, points, lats):
            code = codes[s, :, c : c + lats]
            low, high = code % lats, code // lats
            value = jnp.zeros((cap, lats), jnp.float32)
            for l in range(lons):
                line = jnp.broadcast_to(patch[l : l + 1, :], (cap, lats))
                found = jnp.take_along_axis(line, low, axis=1, mode="promise_in_bounds")
                value = jnp.where(high == l, found, value)
            recs[s, :, c : c + lats] = value

    each(n_own, look_up)
    rec = recs[...].reshape(n_own * cap, points)
    first = rec.astype(jnp.bfloat16)
    rest = rec - first.astype(jnp.float32)
    second = rest.astype(jnp.bfloat16)
    third = (rest - second.astype(jnp.float32)).astype(jnp.bfloat16)
    chosen = select[...]
    out_table[...] = (
        jnp.dot(chosen, first, preferred_element_type=jnp.float32)
        + jnp.dot(chosen, second, preferred_element_type=jnp.float32)
        + jnp.dot(chosen, third, preferred_element_type=jnp.float32)
    )

    stores[2].start()

    def sent(ref, sem):
        pltpu.make_async_copy(ref, ref, sem).wait()

    for way, ref in enumerate(
        (
            cells.at[:, :, 1], cells.at[:, :, lons],
            shell_out.at[:, 0], shell_out.at[:, 1], lat_out.at[:, :, 0], lat_out.at[:, :, 1],
        )
    ):
        guarded(sends[way], lambda: sent(ref, halo_send.at[way]))
    sent(map_out.at[1:n_own], map_send)
    sent(side_out.at[1:n_own], side_send)

    @pl.when(me_s == 0)
    def _():
        for first in range(1, n_all, n_own):
            last = min(first + n_own, n_all)
            sent(mags.at[0 : last - first], mag_send)

    for store in stores:
        store.wait()


def write_out(fields, phi, table, out, out_phi, out_table, held, held_phi, held_table, sems):
    pieces = [(phi, held_phi, out_phi), (table, held_table, out_table)]
    count = fields.shape[0]
    for f in range(0, count, 2):
        span = pl.ds(f, 2)
        pieces.insert(len(pieces) - 2, (fields.at[span], held.at[span], out.at[span]))
    loads = [pltpu.make_async_copy(a, b, sems.at[0, i]) for i, (a, b, _) in enumerate(pieces)]
    stores = [pltpu.make_async_copy(b, c, sems.at[1, i]) for i, (_, b, c) in enumerate(pieces)]
    for load in loads:
        load.start()
    for load, store in zip(loads, stores):
        load.wait()
        store.start()
    for store in stores:
        store.wait()


def shards(plasma_fields, velocity, resistivity, conductance, foot_map, foot_owner, foot_row):
    n_lon, n_sec, n_rad = lax.axis_size("lon"), lax.axis_size("sec"), lax.axis_size("rad")
    n_fields, shells, lons, lats = plasma_fields.shape
    count, points = foot_map.shape
    n_own, n_all, n_groups = n_lon * n_rad, n_lon * n_sec * n_rad, len(GROUPS)
    cap = max(8, 2 * count // n_own)
    sizes = (n_lon, n_sec, n_rad, n_fields, shells, lons, lats, cap)
    f32 = jnp.float32
    dma = pltpu.SemaphoreType.DMA
    hbm = pl.BlockSpec(memory_space=pltpu.HBM)
    results = (
        jax.ShapeDtypeStruct((n_fields, shells * lons, lats), f32),
        jax.ShapeDtypeStruct((lons, lats), f32),
        jax.ShapeDtypeStruct((ROWS_OWN, points), f32),
    )
    made = pl.pallas_call(
        functools.partial(kernel, sizes),
        out_shape=results,
        in_specs=[hbm] * 7,
        out_specs=(hbm,) * 3,
        scratch_shapes=[
            pltpu.VMEM((n_fields, shells * lons, lats), f32),
            pltpu.VMEM((lons, lats), f32),
            pltpu.VMEM((ROWS_OWN, points), f32),
            dma((3,)),
            pltpu.VMEM((n_fields, shells * lons, lats), f32),
            pltpu.VMEM((3, shells * lons, lats), velocity.dtype),
            pltpu.VMEM((shells * lons, lats), resistivity.dtype),
            pltpu.VMEM((lons, lats), f32),
            pltpu.VMEM((count, points), jnp.int32),
            pltpu.VMEM((1, count), jnp.int32),
            pltpu.VMEM((1, count), jnp.int32),
            dma((7,)),
            pltpu.VMEM((4, shells * lons, lats), f32),
            pltpu.VMEM((7, lons, shells, lats), f32),
            pltpu.VMEM((PHASES, n_fields, lons + 2, shells, lats), f32),
            pltpu.VMEM((PHASES, 2, n_fields, lons, 1, lats), f32),
            pltpu.VMEM((PHASES, 2, n_fields, lons, 1, lats), f32),
            pltpu.VMEM((PHASES, n_groups, 2, shells, lats), f32),
            pltpu.VMEM((PHASES, n_groups, 2, shells, lats), f32),
            pltpu.VMEM((n_own, 2, lons, lats), f32),
            pltpu.VMEM((n_own, cap, points), f32),
            pltpu.VMEM((n_own, cap, points), f32),
            pltpu.VMEM((n_own, 8 + lons, count), f32),
            pltpu.VMEM((n_own, 8 + lons, count), f32),
            pltpu.VMEM((n_own, lons, lats), f32),
            pltpu.VMEM((n_own, cap, points), f32),
            pltpu.VMEM((n_own, cap, points), jnp.int32),
            pltpu.VMEM((ROWS_OWN, n_own * cap), jnp.bfloat16),
            dma((6,)),
            dma((PHASES, n_groups, 6)),
            dma,
            dma((n_own,)),
            dma,
            dma((n_own,)),
            dma,
            dma((n_own,)),
        ],
        compiler_params=pltpu.CompilerParams(
            collective_id=0, has_side_effects=True, vmem_limit_bytes=64 * 1024 * 1024
        ),
    )(
        plasma_fields.reshape(n_fields, shells * lons, lats),
        velocity.reshape(3, shells * lons, lats),
        resistivity.reshape(shells * lons, lats),
        conductance,
        foot_map,
        foot_owner.reshape(1, count),
        foot_row.reshape(1, count),
    )
    current, potential, table = pl.pallas_call(
        write_out,
        out_shape=results,
        in_specs=[hbm] * 3,
        out_specs=(hbm,) * 3,
        scratch_shapes=[pltpu.VMEM(r.shape, r.dtype) for r in results] + [dma((2, 2 + n_fields // 2))],
        compiler_params=pltpu.CompilerParams(vmem_limit_bytes=64 * 1024 * 1024),
    )(*made)
    return current.reshape(plasma_fields.shape), potential, table


def solution(mesh):
    in_specs = (
        P(None, "sec", "lon", "rad"),
        P(None, "sec", "lon", "rad"),
        P("sec", "lon", "rad"),
        P("lon", "rad"),
        P(("lon", "sec", "rad"), None),
        P(("lon", "sec", "rad"), None),
        P(("lon", "sec", "rad")),
    )
    out_specs = (P(None, "sec", "lon", "rad"), P("lon", "rad"), P(("lon", "sec", "rad"), None))
    return jax.shard_map(shards, mesh=mesh, in_specs=in_specs, out_specs=out_specs, check_vma=False)
```

```python
import functools

import jax
import jax.numpy as jnp
from jax import lax
from jax.experimental import pallas as pl
from jax.experimental.pallas import tpu as pltpu
from jax.sharding import PartitionSpec as P

PHASES = 4
SWEEPS = 8
ROWS_OWN = 32
COURANT = 0.25
DAMPING = 0.05
RELAX = 0.8
MESH = pl.DeviceIdType.MESH
ORDER = (5, 6, 0, 1, 2, 3, 4, 7)
GROUPS = ((0, 2), (2, 5), (5, 8))


def each(count, body):
    if count <= 16:
        for i in range(count):
            body(i)
    else:
        lax.fori_loop(0, count, lambda i, c: (body(i), c)[1], 0)


def kernel(
    sizes,
    fields_at, vel_at, res_at, cond_at, fmap_at, fowner_at, frow_at,
    end_fields, end_phi, end_table,
    out, out_phi, out_table, store_sem, fields, vel, res, cond, fmap, fowner, frow, load_sem,
    wide, coef, cells, shell_out, shell_in, lat_out, lat_in,
    mags, map_out, map_in, side_out, side_in, phis, recs, codes, select,
    halo_send, halo_recv, mag_send, mag_recv, map_send, map_recv, side_send, side_recv,
):
    n_lon, n_sec, n_rad, n_fields, shells, lons, lats, cap = sizes
    me_l, me_s, me_r = lax.axis_index("lon"), lax.axis_index("sec"), lax.axis_index("rad")
    n_all, n_own = n_lon * n_sec * n_rad, n_lon * n_rad
    me_own = me_l * n_rad + me_r
    me_flat = (me_l * n_sec + me_s) * n_rad + me_r

    loads = [
        pltpu.make_async_copy(src, dst, load_sem.at[i])
        for i, (src, dst) in enumerate(
            (
                (fields_at, fields), (vel_at, vel), (res_at, res), (cond_at, cond),
                (fmap_at, fmap), (fowner_at, fowner), (frow_at, frow),
            )
        )
    ]
    for load in loads:
        load.start()

    def turn(me, by, count):
        return lax.rem(me + by, count)

    def peer(t):
        dl, ds, dr = t // (n_sec * n_rad), (t // n_rad) % n_sec, t % n_rad
        return (turn(me_l, dl, n_lon), turn(me_s, ds, n_sec), turn(me_r, dr, n_rad))

    def mate(t):
        return (turn(me_l, t // n_rad, n_lon), me_s, turn(me_r, t % n_rad, n_rad))

    def others(count, body):
        if count <= 64:
            for t in range(1, count):
                body(t)
        else:
            lax.fori_loop(1, count, lambda t, c: (body(t), c)[1], 0)

    barrier = pltpu.get_barrier_semaphore()
    others(n_all, lambda t: pl.semaphore_signal(barrier, inc=1, device_id=peer(t), device_id_type=MESH))

    lane = lax.broadcasted_iota(jnp.int32, (shells, lats), 1)
    lane3 = lax.broadcasted_iota(jnp.int32, (lons, shells, lats), 2)
    row3 = lax.broadcasted_iota(jnp.int32, (lons, shells, lats), 1)

    def publish(p, g, blocks):
        f0, _ = GROUPS[g]
        low = jnp.zeros((shells, lats), jnp.float32)
        high = jnp.zeros((shells, lats), jnp.float32)
        for i, block in enumerate(blocks):
            f = f0 + i
            cells[p, f, 1 : lons + 1] = block
            shell_out[p, 0, f] = block[:, 0:1, :]
            shell_out[p, 1, f] = block[:, shells - 1 : shells, :]
            for l in range(lons):
                k = i * lons + l
                low = jnp.where(lane == k, pltpu.roll(block[l], k, 1) if k else block[l], low)
                high = jnp.where(lane == k, pltpu.roll(block[l], k + 1, 1), high)
        lat_out[p, g, 0] = low
        lat_out[p, g, 1] = high

    left, right = lax.rem(me_l + n_lon - 1, n_lon), lax.rem(me_l + 1, n_lon)

    def halo(p, g, way):
        f0, f1 = GROUPS[g]
        span = pl.ds(f0, f1 - f0)
        src, dst, to = (
            (lambda: (cells.at[p, span, 1], cells.at[p, span, lons + 1], (left, me_s, me_r))),
            (lambda: (cells.at[p, span, lons], cells.at[p, span, 0], (right, me_s, me_r))),
            (lambda: (shell_out.at[p, 0, span], shell_in.at[p, 1, span], (me_l, me_s - 1, me_r))),
            (lambda: (shell_out.at[p, 1, span], shell_in.at[p, 0, span], (me_l, me_s + 1, me_r))),
            (lambda: (lat_out.at[p, g, 0], lat_in.at[p, g, 1], (me_l, me_s, me_r - 1))),
            (lambda: (lat_out.at[p, g, 1], lat_in.at[p, g, 0], (me_l, me_s, me_r + 1))),
        )[way]()
        return pltpu.make_async_remote_copy(
            src_ref=src, dst_ref=dst, send_sem=halo_send.at[way], recv_sem=halo_recv.at[p, g, way],
            device_id=to, device_id_type=MESH,
        )

    sends = (None, None, me_s > 0, me_s < n_sec - 1, me_r > 0, me_r < n_rad - 1)
    takes = (None, None, me_s < n_sec - 1, me_s > 0, me_r < n_rad - 1, me_r > 0)

    def guarded(cond_value, act):
        if cond_value is None:
            act()
        else:
            pl.when(cond_value)(act)

    def start_halo(p, g):
        for way in (4, 5, 2, 3, 0, 1):
            guarded(sends[way], lambda: halo(p, g, way).start())

    def wait_halo(p, g):
        for way in range(6):
            guarded(takes[way], lambda: halo(p, g, way).wait_recv())

    loads[0].wait()
    for g, (f0, f1) in enumerate(GROUPS):
        blocks = []
        for f in ORDER[f0:f1]:
            blocks.append(jnp.stack([fields[f, pl.ds(l, shells, stride=lons), :] for l in range(lons)]))
        publish(0, g, blocks)

    @pl.when(me_s == 0)
    def _():
        shell_in[:, 0] = jnp.zeros_like(shell_in[:, 0])

    @pl.when(me_s == n_sec - 1)
    def _():
        shell_in[:, 1] = jnp.zeros_like(shell_in[:, 1])

    @pl.when(me_r == 0)
    def _():
        lat_in[:, :, 0] = jnp.zeros_like(lat_in[:, :, 0])

    @pl.when(me_r == n_rad - 1)
    def _():
        lat_in[:, :, 1] = jnp.zeros_like(lat_in[:, :, 1])

    pl.semaphore_wait(barrier, n_all - 1)

    for g in range(len(GROUPS)):
        start_halo(0, g)

    for load in loads[3:]:
        load.wait()
    count, points = fmap.shape
    g_row = lax.broadcasted_iota(jnp.int32, (count, count), 0)
    g_lane = lax.broadcasted_iota(jnp.int32, (count, count), 1)
    owner_l = jnp.broadcast_to(fowner[...].astype(jnp.float32), (count, count))
    row_l = jnp.broadcast_to(frow[...].astype(jnp.float32), (count, count))
    same = g_row == g_lane
    owner_c = jnp.sum(jnp.where(same, owner_l, 0.0), axis=1, keepdims=True)
    row_c = jnp.sum(jnp.where(same, row_l, 0.0), axis=1, keepdims=True)
    alike = owner_c == owner_l
    rank_l = jnp.sum(jnp.where(alike & (g_row < g_lane), 1.0, 0.0), axis=0, keepdims=True)
    rank_c = jnp.sum(jnp.where(alike & (g_row > g_lane), 1.0, 0.0), axis=1, keepdims=True)
    key_l = owner_l[0:1] * float(cap) + rank_l
    key_c = owner_c * float(count) + rank_c
    spot = lax.broadcasted_iota(jnp.int32, (n_own * cap, count), 0).astype(jnp.float32)
    spot_l = g_lane.astype(jnp.float32)
    ids = fmap[...]
    high_part = (ids // lats).astype(jnp.float32).astype(jnp.bfloat16)
    low_part = (ids % lats).astype(jnp.float32).astype(jnp.bfloat16)
    pick = jnp.where(spot == key_l, 1.0, 0.0).astype(jnp.bfloat16)
    highs = jnp.dot(pick, high_part, preferred_element_type=jnp.float32)
    lows = jnp.dot(pick, low_part, preferred_element_type=jnp.float32)
    map_out[...] = (highs * float(lats) + lows).reshape(n_own, cap, points)

    def side_owner(o):
        base = jnp.asarray(o * count, jnp.int32).astype(jnp.float32)
        hit = spot_l + base == key_c
        rows = jnp.sum(jnp.where(hit, row_c + 1.0, 0.0), axis=0, keepdims=True) - 1.0
        side_out[o, 0:8] = jnp.broadcast_to(rows, (8, count))
        side_out[o, 8 : 8 + lons] = cond[...]

    each(n_own, side_owner)
    map_in[me_own] = map_out[me_own]
    side_in[me_own] = side_out[me_own]

    def to_mate(t, src, dst, send, recv):
        l, _, r = mate(t)
        return pltpu.make_async_remote_copy(
            src_ref=src.at[l * n_rad + r], dst_ref=dst.at[me_own], send_sem=send, recv_sem=recv.at[t],
            device_id=(l, me_s, r), device_id_type=MESH,
        )

    def map_copy(t):
        return to_mate(t, map_out, map_in, map_send, map_recv)

    def side_copy(t):
        return to_mate(t, side_out, side_in, side_send, side_recv)

    def start_mate(t):
        side_copy(t).start()
        map_copy(t).start()

    if n_own > 64:
        others(n_own, start_mate)

    loads[1].wait()
    loads[2].wait()
    wide[0:3] = vel[...].astype(jnp.float32)
    wide[3] = res[...].astype(jnp.float32)
    for l in range(lons):
        w = [wide[d, pl.ds(l, shells, stride=lons), :] for d in range(3)]
        r = wide[3, pl.ds(l, shells, stride=lons), :]
        middle = 1.0 - 6.0 * r
        for d in range(3):
            up = COURANT * jnp.maximum(w[d], 0.0)
            down = COURANT * jnp.minimum(w[d], 0.0)
            coef[1 + 2 * d, l] = r + up
            coef[2 + 2 * d, l] = r - down
            middle = middle - (up - down)
        coef[0, l] = middle

    def step(p, g, i):
        f = GROUPS[g][0] + i
        here = cells[p, f, 1 : lons + 1]
        total = coef[0] * here
        total += coef[3] * cells[p, f, 0:lons] + coef[4] * cells[p, f, 2 : lons + 2]
        lower = jnp.where(row3 == 0, shell_in[p, 0, f], pltpu.roll(here, 1, 1))
        upper = jnp.where(row3 == shells - 1, shell_in[p, 1, f], pltpu.roll(here, shells - 1, 1))
        total += coef[1] * lower + coef[2] * upper
        low_edge, high_edge = lat_in[p, g, 0], lat_in[p, g, 1]
        ks = [i * lons + l for l in range(lons)]
        low_edges = jnp.stack([pltpu.roll(low_edge, lats - k, 1) if k else low_edge for k in ks])
        high_edges = jnp.stack([pltpu.roll(high_edge, lats - 1 - k, 1) for k in ks])
        lower = jnp.where(lane3 == 0, low_edges, pltpu.roll(here, 1, 2))
        upper = jnp.where(lane3 == lats - 1, high_edges, pltpu.roll(here, lats - 1, 2))
        return total + coef[5] * lower + coef[6] * upper

    def mag_copy(t):
        return pltpu.make_async_remote_copy(
            src_ref=mags.at[me_own], dst_ref=mags.at[me_own], send_sem=mag_send,
            recv_sem=mag_recv.at[me_own], device_id=peer(t), device_id_type=MESH,
        )

    stores = []

    def store(src, dst):
        copy = pltpu.make_async_copy(src, dst, store_sem.at[len(stores)])
        copy.start()
        stores.append(copy)

    def run(p, g):
        f0, f1 = GROUPS[g]
        wait_halo(p, g)
        blocks = [step(p, g, i) for i in range(f1 - f0)]
        if p < PHASES - 1:
            publish(p + 1, g, blocks)
            start_halo(p + 1, g)
            return
        if g == 0:

            @pl.when(me_s == 0)
            def _():
                for c in range(2):
                    for l in range(lons):
                        mags[me_own, c, l : l + 1, :] = blocks[c][l, 0:1, :]
                others(n_all, lambda t: mag_copy(t).start())

        for i in range(f1 - f0):
            for l in range(lons):
                out[ORDER[f0 + i], pl.ds(l, shells, stride=lons), :] = blocks[i][l]
        for f in ORDER[f0:f1]:
            store(out.at[f], end_fields.at[f])

    for p in range(PHASES - 1):
        for t in range(1 + p, n_own, PHASES - 1) if n_own <= 64 else ():
            start_mate(t)
        run(p, 0)
        run(p, 1)
        if p == PHASES - 2:
            run(p + 1, 0)
        run(p, 2)

    def wait_mate(t):
        side_copy(t).wait_recv()
        map_copy(t).wait_recv()

    others(n_own, wait_mate)

    def whole(get):
        return jnp.concatenate(
            [jnp.concatenate([get(i * n_rad + j) for j in range(n_rad)], axis=1) for i in range(n_lon)], axis=0
        )

    nl, nt = n_lon * lons, n_rad * lats
    t_full = lax.broadcasted_iota(jnp.int32, (nl, nt), 1)

    def lon_up(x):
        return pltpu.roll(x, nl - 1, 0)

    def lon_down(x):
        return pltpu.roll(x, 1, 0)

    def lat_up(x):
        return jnp.where(t_full == nt - 1, 0.0, pltpu.roll(x, nt - 1, 1))

    def lat_down(x):
        return jnp.where(t_full == 0, 0.0, pltpu.roll(x, 1, 1))

    c_full = whole(lambda o: side_in[o, 8 : 8 + lons])
    east = 0.5 * (c_full + lon_up(c_full))
    west = 0.5 * (c_full + lon_down(c_full))
    north = 0.5 * (c_full + lat_up(c_full))
    south = 0.5 * (c_full + lat_down(c_full))
    scale = RELAX / (DAMPING * c_full + east + west + north + south)
    east, west, north, south = east * scale, west * scale, north * scale, south * scale

    rows_at = lax.broadcasted_iota(jnp.int32, (ROWS_OWN, count), 0).astype(jnp.float32)
    per = count // cap
    for b in range(n_own // per if n_own >= per else 1):
        part = jnp.zeros((ROWS_OWN, count), jnp.float32)
        for s in range(b * per, min((b + 1) * per, n_own)):
            one = jnp.where(rows_at == side_in[s, 0:1, :], 1.0, 0.0)
            off = (s * cap) % count
            part += pltpu.roll(one, off, 1) if off else one
        select[:, b * count : (b + 1) * count] = part.astype(jnp.bfloat16)
    codes[...] = map_in[...].astype(jnp.int32)

    def wait_mag(s):
        def act():
            pltpu.make_async_remote_copy(
                src_ref=mags.at[s], dst_ref=mags.at[s], send_sem=mag_send, recv_sem=mag_recv.at[s],
                device_id=(me_l, me_s, me_r), device_id_type=MESH,
            ).wait_recv()

        pl.when((me_s > 0) | (me_own != s))(act)

    each(n_own, wait_mag)

    blon = whole(lambda o: mags[o, 0])
    blat = whole(lambda o: mags[o, 1])
    source = scale * (lon_up(blat) - lon_down(blat) - (lat_up(blon) - lat_down(blon)))
    phi = source
    for _ in range(SWEEPS - 1):
        phi = (
            ((1.0 - RELAX) * phi + source)
            + (east * lon_up(phi) + west * lon_down(phi))
            + (north * lat_up(phi) + south * lat_down(phi))
        )
    for i in range(n_lon):
        for j in range(n_rad):
            phis[i * n_rad + j] = phi[i * lons : (i + 1) * lons, j * lats : (j + 1) * lats]
    out_phi[...] = phis[me_own]
    store(out_phi, end_phi)

    def look_up(s):
        patch = phis[s]
        for c in range(0, points, lats):
            code = codes[s, :, c : c + lats]
            low, high = code % lats, code // lats
            value = jnp.zeros((cap, lats), jnp.float32)
            for l in range(lons):
                line = jnp.broadcast_to(patch[l : l + 1, :], (cap, lats))
                found = jnp.take_along_axis(line, low, axis=1, mode="promise_in_bounds")
                value = jnp.where(high == l, found, value)
            recs[s, :, c : c + lats] = value

    each(n_own, look_up)
    rec = recs[...].reshape(n_own * cap, points)
    first = rec.astype(jnp.bfloat16)
    rest = rec - first.astype(jnp.float32)
    second = rest.astype(jnp.bfloat16)
    third = (rest - second.astype(jnp.float32)).astype(jnp.bfloat16)
    chosen = select[...]
    out_table[...] = (
        jnp.dot(chosen, first, preferred_element_type=jnp.float32)
        + jnp.dot(chosen, second, preferred_element_type=jnp.float32)
        + jnp.dot(chosen, third, preferred_element_type=jnp.float32)
    )

    store(out_table, end_table)

    run(PHASES - 1, 1)
    run(PHASES - 1, 2)

    def sent(ref, sem):
        pltpu.make_async_copy(ref, ref, sem).wait()

    for way, ref in enumerate(
        (
            cells.at[:, :, 1], cells.at[:, :, lons],
            shell_out.at[:, 0], shell_out.at[:, 1], lat_out.at[:, :, 0], lat_out.at[:, :, 1],
        )
    ):
        guarded(sends[way], lambda: sent(ref, halo_send.at[way]))
    sent(map_out.at[1:n_own], map_send)
    sent(side_out.at[1:n_own], side_send)

    @pl.when(me_s == 0)
    def _():
        for first in range(1, n_all, n_own):
            last = min(first + n_own, n_all)
            sent(mags.at[0 : last - first], mag_send)

    for copy in stores:
        copy.wait()


def write_out(fields, phi, table, out, out_phi, out_table, held, held_phi, held_table, sems):
    pieces = [(phi, held_phi, out_phi), (table, held_table, out_table)]
    count = fields.shape[0]
    for f in range(0, count, 2):
        span = pl.ds(f, 2)
        pieces.insert(len(pieces) - 2, (fields.at[span], held.at[span], out.at[span]))
    loads = [pltpu.make_async_copy(a, b, sems.at[0, i]) for i, (a, b, _) in enumerate(pieces)]
    stores = [pltpu.make_async_copy(b, c, sems.at[1, i]) for i, (_, b, c) in enumerate(pieces)]
    for load in loads:
        load.start()
    for load, store in zip(loads, stores):
        load.wait()
        store.start()
    for copy in stores:
        copy.wait()


def shards(plasma_fields, velocity, resistivity, conductance, foot_map, foot_owner, foot_row):
    n_lon, n_sec, n_rad = lax.axis_size("lon"), lax.axis_size("sec"), lax.axis_size("rad")
    n_fields, shells, lons, lats = plasma_fields.shape
    count, points = foot_map.shape
    n_own, n_all, n_groups = n_lon * n_rad, n_lon * n_sec * n_rad, len(GROUPS)
    cap = max(8, 2 * count // n_own)
    sizes = (n_lon, n_sec, n_rad, n_fields, shells, lons, lats, cap)
    f32 = jnp.float32
    dma = pltpu.SemaphoreType.DMA
    hbm = pl.BlockSpec(memory_space=pltpu.HBM)
    results = (
        jax.ShapeDtypeStruct((n_fields, shells * lons, lats), f32),
        jax.ShapeDtypeStruct((lons, lats), f32),
        jax.ShapeDtypeStruct((ROWS_OWN, points), f32),
    )
    made = pl.pallas_call(
        functools.partial(kernel, sizes),
        out_shape=results,
        in_specs=[hbm] * 7,
        out_specs=(hbm,) * 3,
        scratch_shapes=[
            pltpu.VMEM((n_fields, shells * lons, lats), f32),
            pltpu.VMEM((lons, lats), f32),
            pltpu.VMEM((ROWS_OWN, points), f32),
            dma((2 + n_fields,)),
            pltpu.VMEM((n_fields, shells * lons, lats), f32),
            pltpu.VMEM((3, shells * lons, lats), velocity.dtype),
            pltpu.VMEM((shells * lons, lats), resistivity.dtype),
            pltpu.VMEM((lons, lats), f32),
            pltpu.VMEM((count, points), jnp.int32),
            pltpu.VMEM((1, count), jnp.int32),
            pltpu.VMEM((1, count), jnp.int32),
            dma((7,)),
            pltpu.VMEM((4, shells * lons, lats), f32),
            pltpu.VMEM((7, lons, shells, lats), f32),
            pltpu.VMEM((PHASES, n_fields, lons + 2, shells, lats), f32),
            pltpu.VMEM((PHASES, 2, n_fields, lons, 1, lats), f32),
            pltpu.VMEM((PHASES, 2, n_fields, lons, 1, lats), f32),
            pltpu.VMEM((PHASES, n_groups, 2, shells, lats), f32),
            pltpu.VMEM((PHASES, n_groups, 2, shells, lats), f32),
            pltpu.VMEM((n_own, 2, lons, lats), f32),
            pltpu.VMEM((n_own, cap, points), f32),
            pltpu.VMEM((n_own, cap, points), f32),
            pltpu.VMEM((n_own, 8 + lons, count), f32),
            pltpu.VMEM((n_own, 8 + lons, count), f32),
            pltpu.VMEM((n_own, lons, lats), f32),
            pltpu.VMEM((n_own, cap, points), f32),
            pltpu.VMEM((n_own, cap, points), jnp.int32),
            pltpu.VMEM((ROWS_OWN, n_own * cap), jnp.bfloat16),
            dma((6,)),
            dma((PHASES, n_groups, 6)),
            dma,
            dma((n_own,)),
            dma,
            dma((n_own,)),
            dma,
            dma((n_own,)),
        ],
        compiler_params=pltpu.CompilerParams(
            collective_id=0, has_side_effects=True, vmem_limit_bytes=64 * 1024 * 1024
        ),
    )(
        plasma_fields.reshape(n_fields, shells * lons, lats),
        velocity.reshape(3, shells * lons, lats),
        resistivity.reshape(shells * lons, lats),
        conductance,
        foot_map,
        foot_owner.reshape(1, count),
        foot_row.reshape(1, count),
    )
    current, potential, table = pl.pallas_call(
        write_out,
        out_shape=results,
        in_specs=[hbm] * 3,
        out_specs=(hbm,) * 3,
        scratch_shapes=[pltpu.VMEM(r.shape, r.dtype) for r in results] + [dma((2, 2 + n_fields // 2))],
        compiler_params=pltpu.CompilerParams(vmem_limit_bytes=64 * 1024 * 1024),
    )(*made)
    return current.reshape(plasma_fields.shape), potential, table


def solution(mesh):
    in_specs = (
        P(None, "sec", "lon", "rad"),
        P(None, "sec", "lon", "rad"),
        P("sec", "lon", "rad"),
        P("lon", "rad"),
        P(("lon", "sec", "rad"), None),
        P(("lon", "sec", "rad"), None),
        P(("lon", "sec", "rad")),
    )
    out_specs = (P(None, "sec", "lon", "rad"), P("lon", "rad"), P(("lon", "sec", "rad"), None))
    return jax.shard_map(shards, mesh=mesh, in_specs=in_specs, out_specs=out_specs, check_vma=False)
```

```python
import functools

import jax
import jax.numpy as jnp
from jax import lax
from jax.experimental import pallas as pl
from jax.experimental.pallas import tpu as pltpu
from jax.sharding import PartitionSpec as P

PHASES = 4
SWEEPS = 8
ROWS_OWN = 32
COURANT = 0.25
DAMPING = 0.05
RELAX = 0.8
MESH = pl.DeviceIdType.MESH
ORDER = (5, 6, 0, 1, 2, 3, 4, 7)
GROUPS = ((0, 2), (2, 8))


def each(count, body):
    if count <= 16:
        for i in range(count):
            body(i)
    else:
        lax.fori_loop(0, count, lambda i, c: (body(i), c)[1], 0)


def kernel(
    sizes,
    fields_at, vel_at, res_at, cond_at, fmap_at, fowner_at, frow_at,
    end_fields, end_phi, end_table,
    out, out_phi, out_table, store_sem, fields, vel, res, cond, fmap, fowner, frow, load_sem,
    wide, coef, cells, shell_out, shell_in, lat_out, lat_in,
    mags, map_out, map_in, phis, recs, codes, select,
    halo_send, halo_recv, mag_send, mag_recv, map_send, map_recv,
):
    n_lon, n_sec, n_rad, n_fields, shells, lons, lats, cap = sizes
    me_l, me_s, me_r = lax.axis_index("lon"), lax.axis_index("sec"), lax.axis_index("rad")
    n_own = n_lon * n_rad
    me_own = me_l * n_rad + me_r

    loads = [
        pltpu.make_async_copy(src, dst, load_sem.at[i])
        for i, (src, dst) in enumerate(
            (
                (fields_at, fields), (vel_at, vel), (res_at, res), (cond_at, cond),
                (fmap_at, fmap), (fowner_at, fowner), (frow_at, frow),
            )
        )
    ]
    for load in loads:
        load.start()

    def turn(me, by, count):
        return lax.rem(me + by, count)

    def above(t):
        return (me_l, turn(me_s, t, n_sec), me_r)

    def mate(t):
        return (turn(me_l, t // n_rad, n_lon), me_s, turn(me_r, t % n_rad, n_rad))

    def others(count, body):
        if count <= 64:
            for t in range(1, count):
                body(t)
        else:
            lax.fori_loop(1, count, lambda t, c: (body(t), c)[1], 0)

    barrier = pltpu.get_barrier_semaphore()
    others(n_sec, lambda t: pl.semaphore_signal(barrier, inc=1, device_id=above(t), device_id_type=MESH))
    others(n_own, lambda t: pl.semaphore_signal(barrier, inc=1, device_id=mate(t), device_id_type=MESH))

    lane = lax.broadcasted_iota(jnp.int32, (shells, lats), 1)
    lane3 = lax.broadcasted_iota(jnp.int32, (lons, shells, lats), 2)
    row3 = lax.broadcasted_iota(jnp.int32, (lons, shells, lats), 1)

    def publish(p, g, blocks):
        f0, _ = GROUPS[g]
        low = jnp.zeros((shells, lats), jnp.float32)
        high = jnp.zeros((shells, lats), jnp.float32)
        for i, block in enumerate(blocks):
            f = f0 + i
            cells[p, f, 1 : lons + 1] = block
            shell_out[p, 0, f] = block[:, 0:1, :]
            shell_out[p, 1, f] = block[:, shells - 1 : shells, :]
            for l in range(lons):
                k = i * lons + l
                low = jnp.where(lane == k, pltpu.roll(block[l], k, 1) if k else block[l], low)
                high = jnp.where(lane == k, pltpu.roll(block[l], k + 1, 1), high)
        lat_out[p, g, 0] = low
        lat_out[p, g, 1] = high

    left, right = lax.rem(me_l + n_lon - 1, n_lon), lax.rem(me_l + 1, n_lon)

    def halo(p, g, way):
        f0, f1 = GROUPS[g]
        span = pl.ds(f0, f1 - f0)
        src, dst, to = (
            (lambda: (cells.at[p, span, 1], cells.at[p, span, lons + 1], (left, me_s, me_r))),
            (lambda: (cells.at[p, span, lons], cells.at[p, span, 0], (right, me_s, me_r))),
            (lambda: (shell_out.at[p, 0, span], shell_in.at[p, 1, span], (me_l, me_s - 1, me_r))),
            (lambda: (shell_out.at[p, 1, span], shell_in.at[p, 0, span], (me_l, me_s + 1, me_r))),
            (lambda: (lat_out.at[p, g, 0], lat_in.at[p, g, 1], (me_l, me_s, me_r - 1))),
            (lambda: (lat_out.at[p, g, 1], lat_in.at[p, g, 0], (me_l, me_s, me_r + 1))),
        )[way]()
        return pltpu.make_async_remote_copy(
            src_ref=src, dst_ref=dst, send_sem=halo_send.at[way], recv_sem=halo_recv.at[p, g, way],
            device_id=to, device_id_type=MESH,
        )

    sends = (None, None, me_s > 0, me_s < n_sec - 1, me_r > 0, me_r < n_rad - 1)
    takes = (None, None, me_s < n_sec - 1, me_s > 0, me_r < n_rad - 1, me_r > 0)

    def guarded(cond_value, act):
        if cond_value is None:
            act()
        else:
            pl.when(cond_value)(act)

    def start_halo(p, g):
        for way in (4, 5, 2, 3, 0, 1):
            guarded(sends[way], lambda: halo(p, g, way).start())

    def wait_halo(p, g):
        for way in range(6):
            guarded(takes[way], lambda: halo(p, g, way).wait_recv())

    loads[0].wait()
    for g, (f0, f1) in enumerate(GROUPS):
        blocks = []
        for f in ORDER[f0:f1]:
            blocks.append(jnp.stack([fields[f, pl.ds(l, shells, stride=lons), :] for l in range(lons)]))
        publish(0, g, blocks)

    @pl.when(me_s == 0)
    def _():
        shell_in[:, 0] = jnp.zeros_like(shell_in[:, 0])

    @pl.when(me_s == n_sec - 1)
    def _():
        shell_in[:, 1] = jnp.zeros_like(shell_in[:, 1])

    @pl.when(me_r == 0)
    def _():
        lat_in[:, :, 0] = jnp.zeros_like(lat_in[:, :, 0])

    @pl.when(me_r == n_rad - 1)
    def _():
        lat_in[:, :, 1] = jnp.zeros_like(lat_in[:, :, 1])

    pl.semaphore_wait(barrier, n_sec - 1 + n_own - 1)

    for g in range(len(GROUPS)):
        start_halo(0, g)

    for load in loads[3:]:
        load.wait()
    count, points = fmap.shape
    g_row = lax.broadcasted_iota(jnp.int32, (count, count), 0)
    g_lane = lax.broadcasted_iota(jnp.int32, (count, count), 1)
    owner_l = jnp.broadcast_to(fowner[...].astype(jnp.float32), (count, count))
    row_l = jnp.broadcast_to(frow[...].astype(jnp.float32), (count, count))
    same = g_row == g_lane
    owner_c = jnp.sum(jnp.where(same, owner_l, 0.0), axis=1, keepdims=True)
    row_c = jnp.sum(jnp.where(same, row_l, 0.0), axis=1, keepdims=True)
    alike = owner_c == owner_l
    rank_l = jnp.sum(jnp.where(alike & (g_row < g_lane), 1.0, 0.0), axis=0, keepdims=True)
    rank_c = jnp.sum(jnp.where(alike & (g_row > g_lane), 1.0, 0.0), axis=1, keepdims=True)
    key_l = owner_l[0:1] * float(cap) + rank_l
    key_c = owner_c * float(count) + rank_c
    spot = lax.broadcasted_iota(jnp.int32, (n_own * cap, count), 0).astype(jnp.float32)
    spot_l = g_lane.astype(jnp.float32)
    ids = fmap[...]
    high_part = (ids // lats).astype(jnp.float32).astype(jnp.bfloat16)
    low_part = (ids % lats).astype(jnp.float32).astype(jnp.bfloat16)
    pick = jnp.where(spot == key_l, 1.0, 0.0).astype(jnp.bfloat16)
    highs = jnp.dot(pick, high_part, preferred_element_type=jnp.float32)
    lows = jnp.dot(pick, low_part, preferred_element_type=jnp.float32)
    map_out[:, 0:cap, :] = (highs * float(lats) + lows).reshape(n_own, cap, points)

    def side_owner(o):
        base = jnp.asarray(o * count, jnp.int32).astype(jnp.float32)
        hit = spot_l + base == key_c
        rows = jnp.sum(jnp.where(hit, row_c + 1.0, 0.0), axis=0, keepdims=True) - 1.0
        map_out[o, cap : cap + 8, 0:count] = jnp.broadcast_to(rows, (8, count))
        map_out[o, cap : cap + lons, count : count + lats] = cond[...]

    each(n_own, side_owner)
    map_in[me_own] = map_out[me_own]

    def to_mate(t, src, dst, send, recv):
        l, _, r = mate(t)
        return pltpu.make_async_remote_copy(
            src_ref=src.at[l * n_rad + r], dst_ref=dst.at[me_own], send_sem=send, recv_sem=recv.at[t],
            device_id=(l, me_s, r), device_id_type=MESH,
        )

    def map_copy(t):
        return to_mate(t, map_out, map_in, map_send, map_recv)

    def start_mate(t):
        map_copy(t).start()

    if n_own > 64:
        others(n_own, start_mate)

    loads[1].wait()
    loads[2].wait()
    wide[0:3] = vel[...].astype(jnp.float32)
    wide[3] = res[...].astype(jnp.float32)
    for l in range(lons):
        w = [wide[d, pl.ds(l, shells, stride=lons), :] for d in range(3)]
        r = wide[3, pl.ds(l, shells, stride=lons), :]
        middle = 1.0 - 6.0 * r
        for d in range(3):
            up = COURANT * jnp.maximum(w[d], 0.0)
            down = COURANT * jnp.minimum(w[d], 0.0)
            coef[1 + 2 * d, l] = r + up
            coef[2 + 2 * d, l] = r - down
            middle = middle - (up - down)
        coef[0, l] = middle

    def step(p, g, i):
        f = GROUPS[g][0] + i
        here = cells[p, f, 1 : lons + 1]
        total = coef[0] * here
        total += coef[3] * cells[p, f, 0:lons] + coef[4] * cells[p, f, 2 : lons + 2]
        lower = jnp.where(row3 == 0, shell_in[p, 0, f], pltpu.roll(here, 1, 1))
        upper = jnp.where(row3 == shells - 1, shell_in[p, 1, f], pltpu.roll(here, shells - 1, 1))
        total += coef[1] * lower + coef[2] * upper
        low_edge, high_edge = lat_in[p, g, 0], lat_in[p, g, 1]
        ks = [i * lons + l for l in range(lons)]
        low_edges = jnp.stack([pltpu.roll(low_edge, lats - k, 1) if k else low_edge for k in ks])
        high_edges = jnp.stack([pltpu.roll(high_edge, lats - 1 - k, 1) for k in ks])
        lower = jnp.where(lane3 == 0, low_edges, pltpu.roll(here, 1, 2))
        upper = jnp.where(lane3 == lats - 1, high_edges, pltpu.roll(here, lats - 1, 2))
        return total + coef[5] * lower + coef[6] * upper

    def mag_copy(to, sem):
        return pltpu.make_async_remote_copy(
            src_ref=mags.at[me_own], dst_ref=mags.at[me_own], send_sem=mag_send.at[sem],
            recv_sem=mag_recv.at[me_own], device_id=to, device_id_type=MESH,
        )

    stores = []

    def store(src, dst):
        copy = pltpu.make_async_copy(src, dst, store_sem.at[len(stores)])
        copy.start()
        stores.append(copy)

    def run(p, g):
        f0, f1 = GROUPS[g]
        wait_halo(p, g)
        blocks = [step(p, g, i) for i in range(f1 - f0)]
        if p < PHASES - 1:
            publish(p + 1, g, blocks)
            start_halo(p + 1, g)
            return
        if g == 0:

            @pl.when(me_s == 0)
            def _():
                for c in range(2):
                    for l in range(lons):
                        mags[me_own, c, l : l + 1, :] = blocks[c][l, 0:1, :]
                others(n_sec, lambda t: mag_copy(above(t), 0).start())
                others(n_own, lambda t: mag_copy(mate(t), 1).start())

        for i in range(f1 - f0):
            for l in range(lons):
                out[ORDER[f0 + i], pl.ds(l, shells, stride=lons), :] = blocks[i][l]
        for f in ORDER[f0:f1]:
            store(out.at[f], end_fields.at[f])

    for p in range(PHASES - 1):
        for t in range(1 + p, n_own, PHASES - 1) if n_own <= 64 else ():
            start_mate(t)
        for g in range(len(GROUPS)):
            run(p, g)
    run(PHASES - 1, 0)

    others(n_own, lambda t: map_copy(t).wait_recv())

    def whole(get):
        return jnp.concatenate(
            [jnp.concatenate([get(i * n_rad + j) for j in range(n_rad)], axis=1) for i in range(n_lon)], axis=0
        )

    nl, nt = n_lon * lons, n_rad * lats
    t_full = lax.broadcasted_iota(jnp.int32, (nl, nt), 1)

    def lon_up(x):
        return pltpu.roll(x, nl - 1, 0)

    def lon_down(x):
        return pltpu.roll(x, 1, 0)

    def lat_up(x):
        return jnp.where(t_full == nt - 1, 0.0, pltpu.roll(x, nt - 1, 1))

    def lat_down(x):
        return jnp.where(t_full == 0, 0.0, pltpu.roll(x, 1, 1))

    c_full = whole(lambda o: map_in[o, cap : cap + lons, count : count + lats])
    east = 0.5 * (c_full + lon_up(c_full))
    west = 0.5 * (c_full + lon_down(c_full))
    north = 0.5 * (c_full + lat_up(c_full))
    south = 0.5 * (c_full + lat_down(c_full))
    scale = RELAX / (DAMPING * c_full + east + west + north + south)
    east, west, north, south = east * scale, west * scale, north * scale, south * scale

    rows_at = lax.broadcasted_iota(jnp.int32, (ROWS_OWN, count), 0).astype(jnp.float32)
    per = count // cap
    for b in range(n_own // per if n_own >= per else 1):
        part = jnp.zeros((ROWS_OWN, count), jnp.float32)
        for s in range(b * per, min((b + 1) * per, n_own)):
            one = jnp.where(rows_at == map_in[s, cap : cap + 1, 0:count], 1.0, 0.0)
            off = (s * cap) % count
            part += pltpu.roll(one, off, 1) if off else one
        select[:, b * count : (b + 1) * count] = part.astype(jnp.bfloat16)
    codes[...] = map_in[:, 0:cap, :].astype(jnp.int32)

    def wait_mag(s):
        pltpu.make_async_remote_copy(
            src_ref=mags.at[s], dst_ref=mags.at[s], send_sem=mag_send.at[1], recv_sem=mag_recv.at[s],
            device_id=(me_l, me_s, me_r), device_id_type=MESH,
        ).wait_recv()

    @pl.when(me_s > 0)
    def _():
        wait_mag(me_own)
        others(n_own, lambda t: mag_copy(mate(t), 1).start())

    for g in range(1, len(GROUPS)):
        run(PHASES - 1, g)

    def wait_mate(t):
        l, _, r = mate(t)
        wait_mag(l * n_rad + r)

    others(n_own, wait_mate)

    blon = whole(lambda o: mags[o, 0])
    blat = whole(lambda o: mags[o, 1])
    source = scale * (lon_up(blat) - lon_down(blat) - (lat_up(blon) - lat_down(blon)))
    phi = source
    for _ in range(SWEEPS - 1):
        phi = (
            ((1.0 - RELAX) * phi + source)
            + (east * lon_up(phi) + west * lon_down(phi))
            + (north * lat_up(phi) + south * lat_down(phi))
        )
    for i in range(n_lon):
        for j in range(n_rad):
            phis[i * n_rad + j] = phi[i * lons : (i + 1) * lons, j * lats : (j + 1) * lats]
    out_phi[...] = phis[me_own]
    store(out_phi, end_phi)

    def look_up(s):
        patch = phis[s]
        for c in range(0, points, lats):
            code = codes[s, :, c : c + lats]
            low, high = code % lats, code // lats
            value = jnp.zeros((cap, lats), jnp.float32)
            for l in range(lons):
                line = jnp.broadcast_to(patch[l : l + 1, :], (cap, lats))
                found = jnp.take_along_axis(line, low, axis=1, mode="promise_in_bounds")
                value = jnp.where(high == l, found, value)
            recs[s, :, c : c + lats] = value

    each(n_own, look_up)
    rec = recs[...].reshape(n_own * cap, points)
    first = rec.astype(jnp.bfloat16)
    rest = rec - first.astype(jnp.float32)
    second = rest.astype(jnp.bfloat16)
    third = (rest - second.astype(jnp.float32)).astype(jnp.bfloat16)
    chosen = select[...]
    out_table[...] = (
        jnp.dot(chosen, first, preferred_element_type=jnp.float32)
        + jnp.dot(chosen, second, preferred_element_type=jnp.float32)
        + jnp.dot(chosen, third, preferred_element_type=jnp.float32)
    )

    store(out_table, end_table)

    def sent(ref, sem):
        pltpu.make_async_copy(ref, ref, sem).wait()

    for way, ref in enumerate(
        (
            cells.at[:, :, 1], cells.at[:, :, lons],
            shell_out.at[:, 0], shell_out.at[:, 1], lat_out.at[:, :, 0], lat_out.at[:, :, 1],
        )
    ):
        guarded(sends[way], lambda: sent(ref, halo_send.at[way]))
    sent(map_out.at[1:n_own], map_send)
    sent(mags.at[1:n_own], mag_send.at[1])

    @pl.when(me_s == 0)
    def _():
        sent(mags.at[1:n_sec], mag_send.at[0])

    for copy in stores:
        copy.wait()


def write_out(fields, phi, table, out, out_phi, out_table, held, held_phi, held_table, sems):
    pieces = [(phi, held_phi, out_phi), (table, held_table, out_table)]
    count = fields.shape[0]
    for f in range(0, count, 2):
        span = pl.ds(f, 2)
        pieces.insert(len(pieces) - 2, (fields.at[span], held.at[span], out.at[span]))
    loads = [pltpu.make_async_copy(a, b, sems.at[0, i]) for i, (a, b, _) in enumerate(pieces)]
    stores = [pltpu.make_async_copy(b, c, sems.at[1, i]) for i, (_, b, c) in enumerate(pieces)]
    for load in loads:
        load.start()
    for load, store in zip(loads, stores):
        load.wait()
        store.start()
    for copy in stores:
        copy.wait()


def shards(plasma_fields, velocity, resistivity, conductance, foot_map, foot_owner, foot_row):
    n_lon, n_sec, n_rad = lax.axis_size("lon"), lax.axis_size("sec"), lax.axis_size("rad")
    n_fields, shells, lons, lats = plasma_fields.shape
    count, points = foot_map.shape
    n_own, n_groups = n_lon * n_rad, len(GROUPS)
    cap = max(8, 2 * count // n_own)
    sizes = (n_lon, n_sec, n_rad, n_fields, shells, lons, lats, cap)
    f32 = jnp.float32
    dma = pltpu.SemaphoreType.DMA
    hbm = pl.BlockSpec(memory_space=pltpu.HBM)
    results = (
        jax.ShapeDtypeStruct((n_fields, shells * lons, lats), f32),
        jax.ShapeDtypeStruct((lons, lats), f32),
        jax.ShapeDtypeStruct((ROWS_OWN, points), f32),
    )
    made = pl.pallas_call(
        functools.partial(kernel, sizes),
        out_shape=results,
        in_specs=[hbm] * 7,
        out_specs=(hbm,) * 3,
        scratch_shapes=[
            pltpu.VMEM((n_fields, shells * lons, lats), f32),
            pltpu.VMEM((lons, lats), f32),
            pltpu.VMEM((ROWS_OWN, points), f32),
            dma((2 + n_fields,)),
            pltpu.VMEM((n_fields, shells * lons, lats), f32),
            pltpu.VMEM((3, shells * lons, lats), velocity.dtype),
            pltpu.VMEM((shells * lons, lats), resistivity.dtype),
            pltpu.VMEM((lons, lats), f32),
            pltpu.VMEM((count, points), jnp.int32),
            pltpu.VMEM((1, count), jnp.int32),
            pltpu.VMEM((1, count), jnp.int32),
            dma((7,)),
            pltpu.VMEM((4, shells * lons, lats), f32),
            pltpu.VMEM((7, lons, shells, lats), f32),
            pltpu.VMEM((PHASES, n_fields, lons + 2, shells, lats), f32),
            pltpu.VMEM((PHASES, 2, n_fields, lons, 1, lats), f32),
            pltpu.VMEM((PHASES, 2, n_fields, lons, 1, lats), f32),
            pltpu.VMEM((PHASES, n_groups, 2, shells, lats), f32),
            pltpu.VMEM((PHASES, n_groups, 2, shells, lats), f32),
            pltpu.VMEM((n_own, 2, lons, lats), f32),
            pltpu.VMEM((n_own, cap + 8, points), f32),
            pltpu.VMEM((n_own, cap + 8, points), f32),
            pltpu.VMEM((n_own, lons, lats), f32),
            pltpu.VMEM((n_own, cap, points), f32),
            pltpu.VMEM((n_own, cap, points), jnp.int32),
            pltpu.VMEM((ROWS_OWN, n_own * cap), jnp.bfloat16),
            dma((6,)),
            dma((PHASES, n_groups, 6)),
            dma((2,)),
            dma((n_own,)),
            dma,
            dma((n_own,)),
        ],
        compiler_params=pltpu.CompilerParams(
            collective_id=0, has_side_effects=True, vmem_limit_bytes=64 * 1024 * 1024
        ),
    )(
        plasma_fields.reshape(n_fields, shells * lons, lats),
        velocity.reshape(3, shells * lons, lats),
        resistivity.reshape(shells * lons, lats),
        conductance,
        foot_map,
        foot_owner.reshape(1, count),
        foot_row.reshape(1, count),
    )
    current, potential, table = pl.pallas_call(
        write_out,
        out_shape=results,
        in_specs=[hbm] * 3,
        out_specs=(hbm,) * 3,
        scratch_shapes=[pltpu.VMEM(r.shape, r.dtype) for r in results] + [dma((2, 2 + n_fields // 2))],
        compiler_params=pltpu.CompilerParams(vmem_limit_bytes=64 * 1024 * 1024),
    )(*made)
    return current.reshape(plasma_fields.shape), potential, table


def solution(mesh):
    in_specs = (
        P(None, "sec", "lon", "rad"),
        P(None, "sec", "lon", "rad"),
        P("sec", "lon", "rad"),
        P("lon", "rad"),
        P(("lon", "sec", "rad"), None),
        P(("lon", "sec", "rad"), None),
        P(("lon", "sec", "rad")),
    )
    out_specs = (P(None, "sec", "lon", "rad"), P("lon", "rad"), P(("lon", "sec", "rad"), None))
    return jax.shard_map(shards, mesh=mesh, in_specs=in_specs, out_specs=out_specs, check_vma=False)
```

```python
import functools

import jax
import jax.numpy as jnp
from jax import lax
from jax.experimental import pallas as pl
from jax.experimental.pallas import tpu as pltpu
from jax.sharding import PartitionSpec as P

PHASES = 4
SWEEPS = 8
ROWS_OWN = 32
COURANT = 0.25
DAMPING = 0.05
RELAX = 0.8
MESH = pl.DeviceIdType.MESH
ORDER = (5, 6, 0, 1, 2, 3, 4, 7)
GROUPS = ((0, 2), (2, 5), (5, 8))


def each(count, body):
    if count <= 16:
        for i in range(count):
            body(i)
    else:
        lax.fori_loop(0, count, lambda i, c: (body(i), c)[1], 0)


def kernel(
    sizes,
    fields_at, vel_at, res_at, cond_at, fmap_at, fowner_at, frow_at,
    end_fields, end_phi, end_table,
    out, out_phi, out_table, store_sem, fields, vel, res, cond, fmap, fowner, frow, load_sem,
    wide, coef, cells, shell_out, shell_in, lat_out, lat_in,
    mags, map_out, map_in, phis, recs, codes, select,
    halo_send, halo_recv, mag_send, mag_recv, map_send, map_recv,
):
    n_lon, n_sec, n_rad, n_fields, shells, lons, lats, cap = sizes
    me_l, me_s, me_r = lax.axis_index("lon"), lax.axis_index("sec"), lax.axis_index("rad")
    n_own = n_lon * n_rad
    me_own = me_l * n_rad + me_r

    loads = [
        pltpu.make_async_copy(src, dst, load_sem.at[i])
        for i, (src, dst) in enumerate(
            (
                (fields_at, fields), (vel_at, vel), (res_at, res), (cond_at, cond),
                (fmap_at, fmap), (fowner_at, fowner), (frow_at, frow),
            )
        )
    ]
    for load in loads:
        load.start()

    def turn(me, by, count):
        return lax.rem(me + by, count)

    def above(t):
        return (me_l, turn(me_s, t, n_sec), me_r)

    def mate(t):
        return (turn(me_l, t // n_rad, n_lon), me_s, turn(me_r, t % n_rad, n_rad))

    def others(count, body):
        if count <= 64:
            for t in range(1, count):
                body(t)
        else:
            lax.fori_loop(1, count, lambda t, c: (body(t), c)[1], 0)

    barrier = pltpu.get_barrier_semaphore()
    others(n_sec, lambda t: pl.semaphore_signal(barrier, inc=1, device_id=above(t), device_id_type=MESH))
    others(n_own, lambda t: pl.semaphore_signal(barrier, inc=1, device_id=mate(t), device_id_type=MESH))

    lane = lax.broadcasted_iota(jnp.int32, (shells, lats), 1)
    lane3 = lax.broadcasted_iota(jnp.int32, (lons, shells, lats), 2)
    row3 = lax.broadcasted_iota(jnp.int32, (lons, shells, lats), 1)

    def keep(p, g, blocks):
        for i, block in enumerate(blocks):
            cells[p, GROUPS[g][0] + i, 1 : lons + 1] = block

    def pack(p, g, blocks):
        f0, _ = GROUPS[g]
        low = jnp.zeros((shells, lats), jnp.float32)
        high = jnp.zeros((shells, lats), jnp.float32)
        for i, block in enumerate(blocks):
            f = f0 + i
            shell_out[p, 0, f] = block[:, 0:1, :]
            shell_out[p, 1, f] = block[:, shells - 1 : shells, :]
            for l in range(lons):
                k = i * lons + l
                low = jnp.where(lane == k, pltpu.roll(block[l], k, 1) if k else block[l], low)
                high = jnp.where(lane == k, pltpu.roll(block[l], k + 1, 1), high)
        lat_out[p, g, 0] = low
        lat_out[p, g, 1] = high

    left, right = lax.rem(me_l + n_lon - 1, n_lon), lax.rem(me_l + 1, n_lon)

    def halo(p, g, way):
        f0, f1 = GROUPS[g]
        span = pl.ds(f0, f1 - f0)
        src, dst, to = (
            (lambda: (cells.at[p, span, 1], cells.at[p, span, lons + 1], (left, me_s, me_r))),
            (lambda: (cells.at[p, span, lons], cells.at[p, span, 0], (right, me_s, me_r))),
            (lambda: (shell_out.at[p, 0, span], shell_in.at[p, 1, span], (me_l, me_s - 1, me_r))),
            (lambda: (shell_out.at[p, 1, span], shell_in.at[p, 0, span], (me_l, me_s + 1, me_r))),
            (lambda: (lat_out.at[p, g, 0], lat_in.at[p, g, 1], (me_l, me_s, me_r - 1))),
            (lambda: (lat_out.at[p, g, 1], lat_in.at[p, g, 0], (me_l, me_s, me_r + 1))),
        )[way]()
        return pltpu.make_async_remote_copy(
            src_ref=src, dst_ref=dst, send_sem=halo_send.at[way], recv_sem=halo_recv.at[p, g, way],
            device_id=to, device_id_type=MESH,
        )

    sends = (None, None, me_s > 0, me_s < n_sec - 1, me_r > 0, me_r < n_rad - 1)
    takes = (None, None, me_s < n_sec - 1, me_s > 0, me_r < n_rad - 1, me_r > 0)

    def guarded(cond_value, act):
        if cond_value is None:
            act()
        else:
            pl.when(cond_value)(act)

    def start_halo(p, g, ways):
        for way in ways:
            guarded(sends[way], lambda: halo(p, g, way).start())

    def wait_halo(p, g):
        for way in range(6):
            guarded(takes[way], lambda: halo(p, g, way).wait_recv())

    loads[0].wait()
    for g, (f0, f1) in enumerate(GROUPS):
        blocks = []
        for f in ORDER[f0:f1]:
            blocks.append(jnp.stack([fields[f, pl.ds(l, shells, stride=lons), :] for l in range(lons)]))
        keep(0, g, blocks)
        pack(0, g, blocks)

    @pl.when(me_s == 0)
    def _():
        shell_in[:, 0] = jnp.zeros_like(shell_in[:, 0])

    @pl.when(me_s == n_sec - 1)
    def _():
        shell_in[:, 1] = jnp.zeros_like(shell_in[:, 1])

    @pl.when(me_r == 0)
    def _():
        lat_in[:, :, 0] = jnp.zeros_like(lat_in[:, :, 0])

    @pl.when(me_r == n_rad - 1)
    def _():
        lat_in[:, :, 1] = jnp.zeros_like(lat_in[:, :, 1])

    pl.semaphore_wait(barrier, n_sec - 1 + n_own - 1)

    for g in range(len(GROUPS)):
        start_halo(0, g, (0, 1, 4, 5, 2, 3))

    for load in loads[3:]:
        load.wait()
    count, points = fmap.shape
    g_row = lax.broadcasted_iota(jnp.int32, (count, count), 0)
    g_lane = lax.broadcasted_iota(jnp.int32, (count, count), 1)
    owner_l = jnp.broadcast_to(fowner[...].astype(jnp.float32), (count, count))
    row_l = jnp.broadcast_to(frow[...].astype(jnp.float32), (count, count))
    same = g_row == g_lane
    owner_c = jnp.sum(jnp.where(same, owner_l, 0.0), axis=1, keepdims=True)
    row_c = jnp.sum(jnp.where(same, row_l, 0.0), axis=1, keepdims=True)
    alike = owner_c == owner_l
    rank_l = jnp.sum(jnp.where(alike & (g_row < g_lane), 1.0, 0.0), axis=0, keepdims=True)
    rank_c = jnp.sum(jnp.where(alike & (g_row > g_lane), 1.0, 0.0), axis=1, keepdims=True)
    key_l = owner_l[0:1] * float(cap) + rank_l
    key_c = owner_c * float(count) + rank_c
    spot = lax.broadcasted_iota(jnp.int32, (n_own * cap, count), 0).astype(jnp.float32)
    spot_l = g_lane.astype(jnp.float32)
    ids = fmap[...]
    high_part = (ids // lats).astype(jnp.float32).astype(jnp.bfloat16)
    low_part = (ids % lats).astype(jnp.float32).astype(jnp.bfloat16)
    pick = jnp.where(spot == key_l, 1.0, 0.0).astype(jnp.bfloat16)
    highs = jnp.dot(pick, high_part, preferred_element_type=jnp.float32)
    lows = jnp.dot(pick, low_part, preferred_element_type=jnp.float32)
    map_out[:, 0:cap, :] = (highs * float(lats) + lows).reshape(n_own, cap, points)

    def side_owner(o):
        base = jnp.asarray(o * count, jnp.int32).astype(jnp.float32)
        hit = spot_l + base == key_c
        rows = jnp.sum(jnp.where(hit, row_c + 1.0, 0.0), axis=0, keepdims=True) - 1.0
        map_out[o, cap : cap + 8, 0:count] = jnp.broadcast_to(rows, (8, count))
        map_out[o, cap : cap + lons, count : count + lats] = cond[...]

    each(n_own, side_owner)
    map_in[me_own] = map_out[me_own]

    def to_mate(t, src, dst, send, recv):
        l, _, r = mate(t)
        return pltpu.make_async_remote_copy(
            src_ref=src.at[l * n_rad + r], dst_ref=dst.at[me_own], send_sem=send, recv_sem=recv.at[t],
            device_id=(l, me_s, r), device_id_type=MESH,
        )

    def map_copy(t):
        return to_mate(t, map_out, map_in, map_send, map_recv)

    def start_mate(t):
        map_copy(t).start()

    if n_own > 64:
        others(n_own, start_mate)

    loads[1].wait()
    loads[2].wait()
    wide[0:3] = vel[...].astype(jnp.float32)
    wide[3] = res[...].astype(jnp.float32)
    for l in range(lons):
        w = [wide[d, pl.ds(l, shells, stride=lons), :] for d in range(3)]
        r = wide[3, pl.ds(l, shells, stride=lons), :]
        middle = 1.0 - 6.0 * r
        for d in range(3):
            up = COURANT * jnp.maximum(w[d], 0.0)
            down = COURANT * jnp.minimum(w[d], 0.0)
            coef[1 + 2 * d, l] = r + up
            coef[2 + 2 * d, l] = r - down
            middle = middle - (up - down)
        coef[0, l] = middle

    def step(p, g, i):
        f = GROUPS[g][0] + i
        here = cells[p, f, 1 : lons + 1]
        total = coef[0] * here
        total += coef[3] * cells[p, f, 0:lons] + coef[4] * cells[p, f, 2 : lons + 2]
        lower = jnp.where(row3 == 0, shell_in[p, 0, f], pltpu.roll(here, 1, 1))
        upper = jnp.where(row3 == shells - 1, shell_in[p, 1, f], pltpu.roll(here, shells - 1, 1))
        total += coef[1] * lower + coef[2] * upper
        low_edge, high_edge = lat_in[p, g, 0], lat_in[p, g, 1]
        ks = [i * lons + l for l in range(lons)]
        low_edges = jnp.stack([pltpu.roll(low_edge, lats - k, 1) if k else low_edge for k in ks])
        high_edges = jnp.stack([pltpu.roll(high_edge, lats - 1 - k, 1) for k in ks])
        lower = jnp.where(lane3 == 0, low_edges, pltpu.roll(here, 1, 2))
        upper = jnp.where(lane3 == lats - 1, high_edges, pltpu.roll(here, lats - 1, 2))
        return total + coef[5] * lower + coef[6] * upper

    def mag_copy(to, sem):
        return pltpu.make_async_remote_copy(
            src_ref=mags.at[me_own], dst_ref=mags.at[me_own], send_sem=mag_send.at[sem],
            recv_sem=mag_recv.at[me_own], device_id=to, device_id_type=MESH,
        )

    stores = []

    def store(src, dst):
        copy = pltpu.make_async_copy(src, dst, store_sem.at[len(stores)])
        copy.start()
        stores.append(copy)

    def run(p, g):
        f0, f1 = GROUPS[g]
        wait_halo(p, g)
        blocks = [step(p, g, i) for i in range(f1 - f0)]
        if p < PHASES - 1:
            keep(p + 1, g, blocks)
            start_halo(p + 1, g, (0, 1))
            pack(p + 1, g, blocks)
            start_halo(p + 1, g, (4, 5, 2, 3))
            return
        if g == 0:

            @pl.when(me_s == 0)
            def _():
                for c in range(2):
                    for l in range(lons):
                        mags[me_own, c, l : l + 1, :] = blocks[c][l, 0:1, :]
                others(n_sec, lambda t: mag_copy(above(t), 0).start())
                others(n_own, lambda t: mag_copy(mate(t), 1).start())

        for i in range(f1 - f0):
            for l in range(lons):
                out[ORDER[f0 + i], pl.ds(l, shells, stride=lons), :] = blocks[i][l]
        for f in ORDER[f0:f1]:
            store(out.at[f], end_fields.at[f])

    for p in range(PHASES - 1):
        for t in range(1 + p, n_own, PHASES - 1) if n_own <= 64 else ():
            start_mate(t)
        for g in range(len(GROUPS)):
            run(p, g)
    run(PHASES - 1, 0)

    others(n_own, lambda t: map_copy(t).wait_recv())

    def whole(get):
        return jnp.concatenate(
            [jnp.concatenate([get(i * n_rad + j) for j in range(n_rad)], axis=1) for i in range(n_lon)], axis=0
        )

    nl, nt = n_lon * lons, n_rad * lats
    t_full = lax.broadcasted_iota(jnp.int32, (nl, nt), 1)

    def lon_up(x):
        return pltpu.roll(x, nl - 1, 0)

    def lon_down(x):
        return pltpu.roll(x, 1, 0)

    def lat_up(x):
        return jnp.where(t_full == nt - 1, 0.0, pltpu.roll(x, nt - 1, 1))

    def lat_down(x):
        return jnp.where(t_full == 0, 0.0, pltpu.roll(x, 1, 1))

    c_full = whole(lambda o: map_in[o, cap : cap + lons, count : count + lats])
    east = 0.5 * (c_full + lon_up(c_full))
    west = 0.5 * (c_full + lon_down(c_full))
    north = 0.5 * (c_full + lat_up(c_full))
    south = 0.5 * (c_full + lat_down(c_full))
    scale = RELAX / (DAMPING * c_full + east + west + north + south)
    east, west, north, south = east * scale, west * scale, north * scale, south * scale

    rows_at = lax.broadcasted_iota(jnp.int32, (ROWS_OWN, count), 0).astype(jnp.float32)
    per = count // cap
    for b in range(n_own // per if n_own >= per else 1):
        part = jnp.zeros((ROWS_OWN, count), jnp.float32)
        for s in range(b * per, min((b + 1) * per, n_own)):
            one = jnp.where(rows_at == map_in[s, cap : cap + 1, 0:count], 1.0, 0.0)
            off = (s * cap) % count
            part += pltpu.roll(one, off, 1) if off else one
        select[:, b * count : (b + 1) * count] = part.astype(jnp.bfloat16)
    codes[...] = map_in[:, 0:cap, :].astype(jnp.int32)

    def wait_mag(s):
        pltpu.make_async_remote_copy(
            src_ref=mags.at[s], dst_ref=mags.at[s], send_sem=mag_send.at[1], recv_sem=mag_recv.at[s],
            device_id=(me_l, me_s, me_r), device_id_type=MESH,
        ).wait_recv()

    @pl.when(me_s > 0)
    def _():
        wait_mag(me_own)
        others(n_own, lambda t: mag_copy(mate(t), 1).start())

    for g in range(1, len(GROUPS)):
        run(PHASES - 1, g)

    def wait_mate(t):
        l, _, r = mate(t)
        wait_mag(l * n_rad + r)

    others(n_own, wait_mate)

    blon = whole(lambda o: mags[o, 0])
    blat = whole(lambda o: mags[o, 1])
    source = scale * (lon_up(blat) - lon_down(blat) - (lat_up(blon) - lat_down(blon)))
    phi = source
    for _ in range(SWEEPS - 1):
        phi = (
            ((1.0 - RELAX) * phi + source)
            + (east * lon_up(phi) + west * lon_down(phi))
            + (north * lat_up(phi) + south * lat_down(phi))
        )
    for i in range(n_lon):
        for j in range(n_rad):
            phis[i * n_rad + j] = phi[i * lons : (i + 1) * lons, j * lats : (j + 1) * lats]
    out_phi[...] = phis[me_own]
    store(out_phi, end_phi)

    def look_up(s):
        patch = phis[s]
        for c in range(0, points, lats):
            code = codes[s, :, c : c + lats]
            low, high = code % lats, code // lats
            value = jnp.zeros((cap, lats), jnp.float32)
            for l in range(lons):
                line = jnp.broadcast_to(patch[l : l + 1, :], (cap, lats))
                found = jnp.take_along_axis(line, low, axis=1, mode="promise_in_bounds")
                value = jnp.where(high == l, found, value)
            recs[s, :, c : c + lats] = value

    each(n_own, look_up)
    rec = recs[...].reshape(n_own * cap, points)
    first = rec.astype(jnp.bfloat16)
    rest = rec - first.astype(jnp.float32)
    second = rest.astype(jnp.bfloat16)
    third = (rest - second.astype(jnp.float32)).astype(jnp.bfloat16)
    chosen = select[...]
    out_table[...] = (
        jnp.dot(chosen, first, preferred_element_type=jnp.float32)
        + jnp.dot(chosen, second, preferred_element_type=jnp.float32)
        + jnp.dot(chosen, third, preferred_element_type=jnp.float32)
    )

    store(out_table, end_table)

    def sent(ref, sem):
        pltpu.make_async_copy(ref, ref, sem).wait()

    for way, ref in enumerate(
        (
            cells.at[:, :, 1], cells.at[:, :, lons],
            shell_out.at[:, 0], shell_out.at[:, 1], lat_out.at[:, :, 0], lat_out.at[:, :, 1],
        )
    ):
        guarded(sends[way], lambda: sent(ref, halo_send.at[way]))
    sent(map_out.at[1:n_own], map_send)
    sent(mags.at[1:n_own], mag_send.at[1])

    @pl.when(me_s == 0)
    def _():
        sent(mags.at[1:n_sec], mag_send.at[0])

    for copy in stores:
        copy.wait()


def write_out(fields, phi, table, out, out_phi, out_table, held, held_phi, held_table, sems):
    pieces = [(phi, held_phi, out_phi), (table, held_table, out_table)]
    count = fields.shape[0]
    for f in range(0, count, 2):
        span = pl.ds(f, 2)
        pieces.insert(len(pieces) - 2, (fields.at[span], held.at[span], out.at[span]))
    loads = [pltpu.make_async_copy(a, b, sems.at[0, i]) for i, (a, b, _) in enumerate(pieces)]
    stores = [pltpu.make_async_copy(b, c, sems.at[1, i]) for i, (_, b, c) in enumerate(pieces)]
    for load in loads:
        load.start()
    for load, store in zip(loads, stores):
        load.wait()
        store.start()
    for copy in stores:
        copy.wait()


def shards(plasma_fields, velocity, resistivity, conductance, foot_map, foot_owner, foot_row):
    n_lon, n_sec, n_rad = lax.axis_size("lon"), lax.axis_size("sec"), lax.axis_size("rad")
    n_fields, shells, lons, lats = plasma_fields.shape
    count, points = foot_map.shape
    n_own, n_groups = n_lon * n_rad, len(GROUPS)
    cap = max(8, 2 * count // n_own)
    sizes = (n_lon, n_sec, n_rad, n_fields, shells, lons, lats, cap)
    f32 = jnp.float32
    dma = pltpu.SemaphoreType.DMA
    hbm = pl.BlockSpec(memory_space=pltpu.HBM)
    results = (
        jax.ShapeDtypeStruct((n_fields, shells * lons, lats), f32),
        jax.ShapeDtypeStruct((lons, lats), f32),
        jax.ShapeDtypeStruct((ROWS_OWN, points), f32),
    )
    made = pl.pallas_call(
        functools.partial(kernel, sizes),
        out_shape=results,
        in_specs=[hbm] * 7,
        out_specs=(hbm,) * 3,
        scratch_shapes=[
            pltpu.VMEM((n_fields, shells * lons, lats), f32),
            pltpu.VMEM((lons, lats), f32),
            pltpu.VMEM((ROWS_OWN, points), f32),
            dma((2 + n_fields,)),
            pltpu.VMEM((n_fields, shells * lons, lats), f32),
            pltpu.VMEM((3, shells * lons, lats), velocity.dtype),
            pltpu.VMEM((shells * lons, lats), resistivity.dtype),
            pltpu.VMEM((lons, lats), f32),
            pltpu.VMEM((count, points), jnp.int32),
            pltpu.VMEM((1, count), jnp.int32),
            pltpu.VMEM((1, count), jnp.int32),
            dma((7,)),
            pltpu.VMEM((4, shells * lons, lats), f32),
            pltpu.VMEM((7, lons, shells, lats), f32),
            pltpu.VMEM((PHASES, n_fields, lons + 2, shells, lats), f32),
            pltpu.VMEM((PHASES, 2, n_fields, lons, 1, lats), f32),
            pltpu.VMEM((PHASES, 2, n_fields, lons, 1, lats), f32),
            pltpu.VMEM((PHASES, n_groups, 2, shells, lats), f32),
            pltpu.VMEM((PHASES, n_groups, 2, shells, lats), f32),
            pltpu.VMEM((n_own, 2, lons, lats), f32),
            pltpu.VMEM((n_own, cap + 8, points), f32),
            pltpu.VMEM((n_own, cap + 8, points), f32),
            pltpu.VMEM((n_own, lons, lats), f32),
            pltpu.VMEM((n_own, cap, points), f32),
            pltpu.VMEM((n_own, cap, points), jnp.int32),
            pltpu.VMEM((ROWS_OWN, n_own * cap), jnp.bfloat16),
            dma((6,)),
            dma((PHASES, n_groups, 6)),
            dma((2,)),
            dma((n_own,)),
            dma,
            dma((n_own,)),
        ],
        compiler_params=pltpu.CompilerParams(
            collective_id=0, has_side_effects=True, vmem_limit_bytes=64 * 1024 * 1024
        ),
    )(
        plasma_fields.reshape(n_fields, shells * lons, lats),
        velocity.reshape(3, shells * lons, lats),
        resistivity.reshape(shells * lons, lats),
        conductance,
        foot_map,
        foot_owner.reshape(1, count),
        foot_row.reshape(1, count),
    )
    current, potential, table = pl.pallas_call(
        write_out,
        out_shape=results,
        in_specs=[hbm] * 3,
        out_specs=(hbm,) * 3,
        scratch_shapes=[pltpu.VMEM(r.shape, r.dtype) for r in results] + [dma((2, 2 + n_fields // 2))],
        compiler_params=pltpu.CompilerParams(vmem_limit_bytes=64 * 1024 * 1024),
    )(*made)
    return current.reshape(plasma_fields.shape), potential, table


def solution(mesh):
    in_specs = (
        P(None, "sec", "lon", "rad"),
        P(None, "sec", "lon", "rad"),
        P("sec", "lon", "rad"),
        P("lon", "rad"),
        P(("lon", "sec", "rad"), None),
        P(("lon", "sec", "rad"), None),
        P(("lon", "sec", "rad")),
    )
    out_specs = (P(None, "sec", "lon", "rad"), P("lon", "rad"), P(("lon", "sec", "rad"), None))
    return jax.shard_map(shards, mesh=mesh, in_specs=in_specs, out_specs=out_specs, check_vma=False)
```
